32 devices in a mesh: wave: 2 (over y), gy: 4 (over z), gz: 2 (over x), vec: 2 (over core).
Axes of the slice: x: 2, y: 2, z: 4, core: 2. Of those that a mesh axis runs over, the one named last changes fastest.
Arguments:
- forcing: float32 [8, 8, 512, 1024], P(('wave', 'vec'), None, 'gy', 'gz'), parts along dimension 0, may hold values from -6 to 6
- wavenumber: float32 [2], P('wave'), parts along dimension 0, may hold values from 0.5 to 2
- mean_flow: float32 [9, 512, 1024], P(None, 'gy', 'gz'), may hold values from -3 to 3
- viscosity: float32 [512, 1024], P('gy', 'gz'), may hold values from 0.05 to 0.5
- viscosity_slope: float32 [2, 512, 1024], P(None, 'gy', 'gz'), may hold values from -1.8 to 1.8
Outputs:
- response: float32 [8, 8, 512, 1024], P(('wave', 'vec'), None, 'gy', 'gz'), parts along dimension 0
The draws below stay inside these ranges and needn't reach their ends.
There are 2 independent parts, one for each index of `wave`. The reference program is written for one: setup_inputs(seed, part) draws one part's arguments, and reference() takes and returns one part's arrays. A program takes and returns all parts, laid end to end along the dimension named above; an argument that names none is the same for every part. Nothing has to cross between parts.
All inputs are finite; a program needn't handle non-finite values.
Results may differ from the reference program's by a relative error of at most 0.00005.
Values sent between devices are 32-bit elements; how exact they have to be, the bound alone decides.
A program may use at most 128 MiB of HBM per device.

```python
import math
import jax
import jax.numpy as jnp
from jax import lax

VECS = 4
NY = 512
NZ = 1024


def block_scale(rng, shape, cuts, low, largest):
    level = 1.0
    for dim, shards_of in cuts:
        steps = jax.random.uniform(jax.random.fold_in(jax.random.fold_in(rng, 6), dim), (shards_of,), jnp.float32, low / len(cuts), largest / len(cuts))
        level = level * jnp.repeat(jnp.exp(steps), shape[dim] // shards_of).reshape((-1,) + (1,) * (len(shape) - 1 - dim))
    return level


def noise(stream_key, extent, scale, limit, pieces=(), kind=jnp.bfloat16):
    drawn = scale * jax.random.normal(stream_key, extent, jnp.float32)
    if pieces:
        drawn = drawn * block_scale(stream_key, extent, pieces, -0.22, 0.18)
    return jnp.clip(drawn, -limit, limit).astype(kind)


def setup_inputs(seed: int = 0, part: int = 0) -> dict:
    keys = jax.random.split(jax.random.key(seed), 6)
    part_keys = jax.random.split(jax.random.fold_in(keys[5], part), 6)
    return {
        "forcing": noise(part_keys[0], (VECS, 8, NY, NZ), 1.0, 6.0, ((0, 2), (2, 4), (3, 2)), jnp.float32),
        "wavenumber": jnp.clip(jax.random.uniform(part_keys[1], (1,), jnp.float32, 0.5, 2.0), 0.5, 2.0),
        "mean_flow": noise(keys[2], (9, NY, NZ), 0.5, 3.0, ((1, 4), (2, 2)), jnp.float32),
        "viscosity": jnp.clip(jnp.exp(math.log(0.5) - 2.3025851 * jax.random.uniform(keys[3], (NY, NZ), jnp.float32) ** block_scale(keys[3], (NY, NZ), ((0, 4), (1, 2)), -0.2, 0.2)), 0.05, 0.5),
        "viscosity_slope": noise(keys[4], (2, NY, NZ), 0.3, 1.8, ((1, 4), (2, 2)), jnp.float32),
    }


precise = lax.Precision.HIGHEST


def angle_table(points):
    last_index = points - 1
    row_index = jnp.arange(points, dtype=jnp.int32)[:, None]
    col_index = jnp.arange(points, dtype=jnp.int32)[None, :]
    unit = math.pi / (2.0 * last_index)
    sine_row = jnp.sin(2.0 * unit * jnp.minimum(row_index, last_index - row_index).astype(jnp.float32))
    total = row_index + col_index
    half_sum = jnp.sin(unit * jnp.minimum(total, 2 * last_index - total).astype(jnp.float32))
    half_diff = jnp.sin(unit * (row_index - col_index).astype(jnp.float32))
    parity = (1 - 2 * (total % 2)).astype(jnp.float32)
    weight = jnp.where((col_index == 0) | (col_index == last_index), 0.5, 1.0).astype(jnp.float32)
    same = row_index == col_index
    denominator = jnp.where(same, 1.0, 2.0 * half_sum * half_diff)
    offdiag = jnp.where(same, 0.0, (math.pi / last_index) * sine_row * parity * weight / denominator)
    diagonal = -jnp.sum(offdiag, axis=1)
    return offdiag + jnp.diag(diagonal)


def rotate(values):
    return jnp.stack((-values[..., 1, :, :], values[..., 0, :, :]), axis=-3)


def apply_operator(forcing, grad_y, curve_y, grad_z, curve_z, streamwise, mean_flow, viscosity, viscosity_slope):
    full_shape = forcing.shape
    split_shape = full_shape[:-3] + (4, 2) + full_shape[-2:]
    source = forcing.reshape(split_shape)
    grad_y = grad_y.reshape(split_shape)
    curve_y = curve_y.reshape(split_shape)
    grad_z = grad_z.reshape(split_shape)
    curve_z = curve_z.reshape(split_shape)
    velocity = source[..., :3, :, :, :]
    advection = streamwise * mean_flow[0] * rotate(velocity) + mean_flow[1] * grad_y[..., :3, :, :, :] + mean_flow[2] * grad_z[..., :3, :, :, :]
    slope_y = jnp.stack((mean_flow[3], mean_flow[5], mean_flow[7]))[:, None]
    slope_z = jnp.stack((mean_flow[4], mean_flow[6], mean_flow[8]))[:, None]
    produce = slope_y * source[..., 1:2, :, :, :] + slope_z * source[..., 2:3, :, :, :]
    diffuse = viscosity * (curve_y[..., :3, :, :, :] + curve_z[..., :3, :, :, :] - streamwise * streamwise * velocity)
    diffuse = diffuse + viscosity_slope[0] * grad_y[..., :3, :, :, :] + viscosity_slope[1] * grad_z[..., :3, :, :, :]
    pressure = jnp.stack((streamwise * rotate(source[..., 3, :, :, :]), grad_y[..., 3, :, :, :], grad_z[..., 3, :, :, :]), axis=-4)
    momentum = -advection - produce + diffuse - pressure
    continuity = streamwise * rotate(source[..., 0, :, :, :]) + grad_y[..., 1, :, :, :] + grad_z[..., 2, :, :, :]
    action = jnp.concatenate((momentum, continuity[..., None, :, :, :]), axis=-4)
    return action.reshape(full_shape)


def reference(forcing, wavenumber, mean_flow, viscosity, viscosity_slope):
    table_y = angle_table(NY)
    table_z = angle_table(NZ)
    streamwise = wavenumber[0]

    def one_vector(vector):
        grad_y = jnp.einsum('ij,cjz->ciz', table_y, vector, precision=precise)
        curve_y = jnp.einsum('ij,cjz->ciz', table_y, grad_y, precision=precise)
        grad_z = jnp.einsum('cyj,ij->cyi', vector, table_z, precision=precise)
        curve_z = jnp.einsum('cyj,ij->cyi', grad_z, table_z, precision=precise)
        return apply_operator(vector, grad_y, curve_y, grad_z, curve_z, streamwise, mean_flow, viscosity, viscosity_slope)

    action = lax.map(one_vector, forcing)
    y_signs = jnp.array([1.0, 1.0, -1.0, -1.0, 1.0, 1.0, 1.0, 1.0], dtype=jnp.float32)[:, None, None]
    z_signs = jnp.array([1.0, 1.0, 1.0, 1.0, -1.0, -1.0, 1.0, 1.0], dtype=jnp.float32)[:, None, None]
    half_y = 0.5 * (action + y_signs * jnp.flip(action, axis=-2))
    return 0.5 * (half_y + z_signs * jnp.flip(half_y, axis=-1))
```

```python
import math

import jax
import jax.numpy as jnp
from jax import lax
from jax.sharding import PartitionSpec as P

precise = lax.Precision.HIGHEST


def angle_table(points):
    last_index = points - 1
    row_index = jnp.arange(points, dtype=jnp.int32)[:, None]
    col_index = jnp.arange(points, dtype=jnp.int32)[None, :]
    unit = math.pi / (2.0 * last_index)
    sine_row = jnp.sin(
        2.0 * unit * jnp.minimum(row_index, last_index - row_index).astype(jnp.float32)
    )
    total = row_index + col_index
    half_sum = jnp.sin(unit * jnp.minimum(total, 2 * last_index - total).astype(jnp.float32))
    half_diff = jnp.sin(unit * (row_index - col_index).astype(jnp.float32))
    parity = (1 - 2 * (total % 2)).astype(jnp.float32)
    weight = jnp.where((col_index == 0) | (col_index == last_index), 0.5, 1.0).astype(jnp.float32)
    same = row_index == col_index
    denominator = jnp.where(same, 1.0, 2.0 * half_sum * half_diff)
    offdiag = jnp.where(same, 0.0, math.pi / last_index * sine_row * parity * weight / denominator)
    diagonal = -jnp.sum(offdiag, axis=1)
    return offdiag + jnp.diag(diagonal)


def rotate(values):
    return jnp.stack((-values[..., 1, :, :], values[..., 0, :, :]), axis=-3)


def apply_operator(
    forcing, grad_y, curve_y, grad_z, curve_z, streamwise, mean_flow, viscosity, viscosity_slope
):
    full_shape = forcing.shape
    split_shape = full_shape[:-3] + (4, 2) + full_shape[-2:]
    source = forcing.reshape(split_shape)
    grad_y = grad_y.reshape(split_shape)
    curve_y = curve_y.reshape(split_shape)
    grad_z = grad_z.reshape(split_shape)
    curve_z = curve_z.reshape(split_shape)
    velocity = source[..., :3, :, :, :]
    advection = (
        streamwise * mean_flow[0] * rotate(velocity)
        + mean_flow[1] * grad_y[..., :3, :, :, :]
        + mean_flow[2] * grad_z[..., :3, :, :, :]
    )
    slope_y = jnp.stack((mean_flow[3], mean_flow[5], mean_flow[7]))[:, None]
    slope_z = jnp.stack((mean_flow[4], mean_flow[6], mean_flow[8]))[:, None]
    produce = slope_y * source[..., 1:2, :, :, :] + slope_z * source[..., 2:3, :, :, :]
    diffuse = viscosity * (
        curve_y[..., :3, :, :, :] + curve_z[..., :3, :, :, :] - streamwise * streamwise * velocity
    )
    diffuse = (
        diffuse
        + viscosity_slope[0] * grad_y[..., :3, :, :, :]
        + viscosity_slope[1] * grad_z[..., :3, :, :, :]
    )
    pressure = jnp.stack(
        (
            streamwise * rotate(source[..., 3, :, :, :]),
            grad_y[..., 3, :, :, :],
            grad_z[..., 3, :, :, :],
        ),
        axis=-4,
    )
    momentum = -advection - produce + diffuse - pressure
    continuity = (
        streamwise * rotate(source[..., 0, :, :, :])
        + grad_y[..., 1, :, :, :]
        + grad_z[..., 2, :, :, :]
    )
    action = jnp.concatenate((momentum, continuity[..., None, :, :, :]), axis=-4)
    return action.reshape(full_shape)


def mirror_rows(values):
    groups = lax.axis_size("gy")
    first_pass = lax.all_to_all(values, "gy", split_axis=1, concat_axis=1, tiled=True)
    second_pass = lax.all_to_all(
        jnp.flip(first_pass, 1), "gy", split_axis=1, concat_axis=1, tiled=True
    )
    fields, rows_local, cols_local = second_pass.shape
    blocks = second_pass.reshape(fields, groups, rows_local // groups, cols_local)
    return jnp.flip(blocks, 1).reshape(fields, rows_local, cols_local)


def mirror_cols(values):
    groups = lax.axis_size("gz")
    first_pass = lax.all_to_all(values, "gz", split_axis=2, concat_axis=2, tiled=True)
    second_pass = lax.all_to_all(
        jnp.flip(first_pass, 2), "gz", split_axis=2, concat_axis=2, tiled=True
    )
    fields, rows_local, cols_local = second_pass.shape
    blocks = second_pass.reshape(fields, rows_local, groups, cols_local // groups)
    return jnp.flip(blocks, 2).reshape(fields, rows_local, cols_local)


def shards(forcing, wavenumber, mean_flow, viscosity, viscosity_slope):
    vectors, components, rows_local, cols_local = forcing.shape
    rows_total = rows_local * lax.axis_size("gy")
    cols_total = cols_local * lax.axis_size("gz")
    table_y = angle_table(rows_total)
    table_z = angle_table(cols_total)
    flattened = forcing.reshape(vectors * components, rows_local, cols_local)
    first = jnp.einsum(
        "ij,fjk->fik",
        table_y,
        lax.all_to_all(flattened, "gy", split_axis=0, concat_axis=1, tiled=True),
        precision=precise,
    )
    second = jnp.einsum("ij,fjk->fik", table_y, first, precision=precise)
    grad_y = lax.all_to_all(first, "gy", split_axis=1, concat_axis=0, tiled=True)
    curve_y = lax.all_to_all(second, "gy", split_axis=1, concat_axis=0, tiled=True)
    own_start = lax.axis_index("gz") * cols_local
    own_rows = lax.dynamic_slice_in_dim(table_z, own_start, cols_local, 0)
    own_second = jnp.dot(own_rows, table_z, precision=precise, preferred_element_type=jnp.float32)
    piece = lax.all_gather(flattened, "gz", axis=2, tiled=True)
    grad_z = jnp.einsum("fyj,ij->fyi", piece, own_rows, precision=precise)
    curve_z = jnp.einsum("fyj,ij->fyi", piece, own_second, precision=precise)
    full_shape = forcing.shape
    action = apply_operator(
        forcing,
        grad_y.reshape(full_shape),
        curve_y.reshape(full_shape),
        grad_z.reshape(full_shape),
        curve_z.reshape(full_shape),
        wavenumber[0],
        mean_flow,
        viscosity,
        viscosity_slope,
    )
    y_signs = jnp.array([1.0, 1.0, -1.0, -1.0, 1.0, 1.0, 1.0, 1.0], dtype=jnp.float32)[
        :, None, None
    ]
    z_signs = jnp.array([1.0, 1.0, 1.0, 1.0, -1.0, -1.0, 1.0, 1.0], dtype=jnp.float32)[
        :, None, None
    ]
    flat_shape = (vectors * components, rows_local, cols_local)
    mirrored = mirror_rows(action.reshape(flat_shape)).reshape(full_shape)
    half_y = 0.5 * (action + y_signs * mirrored)
    mirrored = mirror_cols(half_y.reshape(flat_shape)).reshape(full_shape)
    return 0.5 * (half_y + z_signs * mirrored)


quick = lax.Precision.HIGH
Y_SIGNS = (1.0, 1.0, -1.0, -1.0, 1.0, 1.0, 1.0, 1.0)
Z_SIGNS = (1.0, 1.0, 1.0, 1.0, -1.0, -1.0, 1.0, 1.0)


def signed(values, signs):
    return jnp.stack([values[k] if signs[k] > 0 else -values[k] for k in range(8)])


def parity_tables(points):
    half = points // 2
    rows = angle_table(points)[:half]
    near, far = rows[:, :half], jnp.flip(rows[:, half:], 1)
    even, odd = near + far, near - far
    second_even = jnp.dot(odd, even, precision=precise)
    second_odd = jnp.dot(even, odd, precision=precise)
    return even, odd, second_even, second_odd


def times_i(pair):
    return jnp.stack((-pair[1], pair[0]))


def action_along_z(source, grad, curve, streamwise, coefs):
    u, v, w, p = (source[2 * k : 2 * k + 2] for k in range(4))
    stream, advect, uy, uz, vy, vz, wy, wz, nu = (coefs[k] for k in range(9))
    out = []
    for k, (c, sy, sz) in enumerate(((u, uy, uz), (v, vy, vz), (w, wy, wz))):
        term = (
            advect * grad[2 * k : 2 * k + 2]
            - streamwise * stream * times_i(c)
            - (sy * v + sz * w)
            + nu * (curve[2 * k : 2 * k + 2] - streamwise * streamwise * c)
        )
        if k == 0:
            term = term - streamwise * times_i(p)
        if k == 2:
            term = term - grad[6:8]
        out.append(term)
    out.append(streamwise * times_i(u) + grad[4:6])
    return jnp.concatenate(out)


def action_along_y(grad, curve, advect, nu):
    first = advect * grad[:6] + nu * curve
    return jnp.concatenate((first[:2], first[2:4] - grad[6:8], first[4:6], grad[2:4]))


def paired(values, swap):
    other = lax.ppermute(values, "gz", [(0, 1), (1, 0)])
    return order_halves(values, other, swap)


def order_halves(own, other, swap):
    return jnp.where(swap, other, own), jnp.flip(jnp.where(swap, own, other), -1)


def paired_shards(forcing, wavenumber, mean_flow, viscosity, viscosity_slope):
    vectors, components, rows_local, cols_local = forcing.shape
    rows_total = rows_local * lax.axis_size("gy")
    half_rows = rows_total // 2
    side = lax.axis_index("gz")
    swap = side == 1
    streamwise = wavenumber[0]
    own = lax.dynamic_index_in_dim(forcing, side, 0, keepdims=False)
    give = lax.dynamic_index_in_dim(forcing, 1 - side, 0, keepdims=False)
    got = lax.ppermute(give, "gz", [(0, 1), (1, 0)])
    near, far = order_halves(own, got, swap)
    lines = lax.all_to_all(
        jnp.stack((near, far)), "gy", split_axis=3, concat_axis=2, tiled=True
    )

    coefs = jnp.concatenate(
        (
            mean_flow[0:1],
            viscosity_slope[1:2] - mean_flow[2:3],
            mean_flow[3:9],
            viscosity[None],
            viscosity_slope[0:1] - mean_flow[1:2],
        )
    )
    copies = lax.axis_size("wave") * lax.axis_size("vec")
    share_rows = rows_local // copies
    share = lax.axis_index("wave") * lax.axis_size("vec") + lax.axis_index("vec")
    piece = lax.dynamic_slice_in_dim(coefs, share * share_rows, share_rows, 1)
    piece = lax.ppermute(piece, "gz", [(0, 1), (1, 0)])
    other = lax.all_gather(piece, ("wave", "vec"), axis=1, tiled=True)
    near_coefs, far_coefs = order_halves(coefs, other, swap)
    line_coefs = lax.all_to_all(
        jnp.stack((near_coefs[8:], far_coefs[8:])), "gy", split_axis=3, concat_axis=2, tiled=True
    )

    even, odd, second_even, second_odd = parity_tables(2 * cols_local)
    source_even, source_odd = 0.5 * (near + far), 0.5 * (near - far)

    def along_z(values, table):
        return jnp.einsum("cyj,ij->cyi", values, table, precision=quick)

    grad_even, grad_odd = along_z(source_even, even), along_z(source_odd, odd)
    curve_even = along_z(source_even[:6], second_even)
    curve_odd = along_z(source_odd[:6], second_odd)
    near_action = action_along_z(
        near, grad_odd + grad_even, curve_even + curve_odd, streamwise, near_coefs
    )
    far_action = action_along_z(
        far, grad_odd - grad_even, curve_even - curve_odd, streamwise, far_coefs
    )
    z_part = 0.5 * (near_action + signed(far_action, Z_SIGNS))
    z_part = lax.all_to_all(z_part, "gy", split_axis=2, concat_axis=1, tiled=True)

    even, odd, second_even, second_odd = parity_tables(rows_total)
    top, bottom = lines[:, :, :half_rows], jnp.flip(lines[:, :, half_rows:], 2)
    source_even, source_odd = 0.5 * (top + bottom), 0.5 * (top - bottom)

    def along_y(values, table):
        return jnp.einsum("ij,scjk->scik", table, values, precision=quick)

    grad_even, grad_odd = along_y(source_even, even), along_y(source_odd, odd)
    curve_even = along_y(source_even[:, :6], second_even)
    curve_odd = along_y(source_odd[:, :6], second_odd)
    top_coefs, bottom_coefs = line_coefs[:, :, :half_rows], jnp.flip(line_coefs[:, :, half_rows:], 2)
    halves = []
    for k in range(2):
        top_action = action_along_y(
            grad_odd[k] + grad_even[k],
            curve_even[k] + curve_odd[k],
            top_coefs[k, 1],
            top_coefs[k, 0],
        )
        bottom_action = action_along_y(
            grad_odd[k] - grad_even[k],
            curve_even[k] - curve_odd[k],
            bottom_coefs[k, 1],
            bottom_coefs[k, 0],
        )
        halves.append(0.5 * (top_action + signed(bottom_action, Y_SIGNS)))
    y_part = 0.5 * (halves[0] + signed(halves[1], Z_SIGNS))
    bottom = jnp.flip(z_part[:, half_rows:], 1)
    quarter = y_part + 0.5 * (z_part[:, :half_rows] + signed(bottom, Y_SIGNS))
    whole = jnp.concatenate((quarter, signed(jnp.flip(quarter, 1), Y_SIGNS)), 1)
    result = lax.all_to_all(whole, "gy", split_axis=1, concat_axis=2, tiled=True)
    mirrored = signed(jnp.flip(result, 2), Z_SIGNS)
    keep = jnp.where(swap, mirrored, result)
    got = lax.ppermute(jnp.where(swap, result, mirrored), "gz", [(0, 1), (1, 0)])
    return jnp.stack((jnp.where(swap, got, keep), jnp.where(swap, keep, got)))


def shards_of(mesh):
    def run(forcing, *others):
        vectors, rows_local = forcing.shape[0], forcing.shape[2]
        copies = mesh.shape["wave"] * mesh.shape["vec"]
        fits = mesh.shape["gz"] == 2 and vectors == 2 and mesh.shape["gy"] % 2 == 0
        if fits and rows_local % (8 * copies) == 0:
            return paired_shards(forcing, *others)
        return shards(forcing, *others)

    return run


def solution(mesh):
    placed = (
        P(("wave", "vec"), None, "gy", "gz"),
        P("wave"),
        P(None, "gy", "gz"),
        P("gy", "gz"),
        P(None, "gy", "gz"),
    )
    return jax.shard_map(
        shards_of(mesh),
        mesh=mesh,
        in_specs=placed,
        out_specs=P(("wave", "vec"), None, "gy", "gz"),
        check_vma=False,
    )
```

```python
import functools
import math

import jax
import jax.numpy as jnp
from jax import lax
from jax.experimental import pallas as pl
from jax.experimental.pallas import tpu as pltpu
from jax.sharding import PartitionSpec as P

precise = lax.Precision.HIGHEST


def angle_table(points):
    last_index = points - 1
    row_index = jnp.arange(points, dtype=jnp.int32)[:, None]
    col_index = jnp.arange(points, dtype=jnp.int32)[None, :]
    unit = math.pi / (2.0 * last_index)
    sine_row = jnp.sin(
        2.0 * unit * jnp.minimum(row_index, last_index - row_index).astype(jnp.float32)
    )
    total = row_index + col_index
    half_sum = jnp.sin(unit * jnp.minimum(total, 2 * last_index - total).astype(jnp.float32))
    half_diff = jnp.sin(unit * (row_index - col_index).astype(jnp.float32))
    parity = (1 - 2 * (total % 2)).astype(jnp.float32)
    weight = jnp.where((col_index == 0) | (col_index == last_index), 0.5, 1.0).astype(jnp.float32)
    same = row_index == col_index
    denominator = jnp.where(same, 1.0, 2.0 * half_sum * half_diff)
    offdiag = jnp.where(same, 0.0, math.pi / last_index * sine_row * parity * weight / denominator)
    diagonal = -jnp.sum(offdiag, axis=1)
    return offdiag + jnp.diag(diagonal)


def rotate(values):
    return jnp.stack((-values[..., 1, :, :], values[..., 0, :, :]), axis=-3)


def apply_operator(
    forcing, grad_y, curve_y, grad_z, curve_z, streamwise, mean_flow, viscosity, viscosity_slope
):
    full_shape = forcing.shape
    split_shape = full_shape[:-3] + (4, 2) + full_shape[-2:]
    source = forcing.reshape(split_shape)
    grad_y = grad_y.reshape(split_shape)
    curve_y = curve_y.reshape(split_shape)
    grad_z = grad_z.reshape(split_shape)
    curve_z = curve_z.reshape(split_shape)
    velocity = source[..., :3, :, :, :]
    advection = (
        streamwise * mean_flow[0] * rotate(velocity)
        + mean_flow[1] * grad_y[..., :3, :, :, :]
        + mean_flow[2] * grad_z[..., :3, :, :, :]
    )
    slope_y = jnp.stack((mean_flow[3], mean_flow[5], mean_flow[7]))[:, None]
    slope_z = jnp.stack((mean_flow[4], mean_flow[6], mean_flow[8]))[:, None]
    produce = slope_y * source[..., 1:2, :, :, :] + slope_z * source[..., 2:3, :, :, :]
    diffuse = viscosity * (
        curve_y[..., :3, :, :, :] + curve_z[..., :3, :, :, :] - streamwise * streamwise * velocity
    )
    diffuse = (
        diffuse
        + viscosity_slope[0] * grad_y[..., :3, :, :, :]
        + viscosity_slope[1] * grad_z[..., :3, :, :, :]
    )
    pressure = jnp.stack(
        (
            streamwise * rotate(source[..., 3, :, :, :]),
            grad_y[..., 3, :, :, :],
            grad_z[..., 3, :, :, :],
        ),
        axis=-4,
    )
    momentum = -advection - produce + diffuse - pressure
    continuity = (
        streamwise * rotate(source[..., 0, :, :, :])
        + grad_y[..., 1, :, :, :]
        + grad_z[..., 2, :, :, :]
    )
    action = jnp.concatenate((momentum, continuity[..., None, :, :, :]), axis=-4)
    return action.reshape(full_shape)


def mirror_rows(values):
    groups = lax.axis_size("gy")
    first_pass = lax.all_to_all(values, "gy", split_axis=1, concat_axis=1, tiled=True)
    second_pass = lax.all_to_all(
        jnp.flip(first_pass, 1), "gy", split_axis=1, concat_axis=1, tiled=True
    )
    fields, rows_local, cols_local = second_pass.shape
    blocks = second_pass.reshape(fields, groups, rows_local // groups, cols_local)
    return jnp.flip(blocks, 1).reshape(fields, rows_local, cols_local)


def mirror_cols(values):
    groups = lax.axis_size("gz")
    first_pass = lax.all_to_all(values, "gz", split_axis=2, concat_axis=2, tiled=True)
    second_pass = lax.all_to_all(
        jnp.flip(first_pass, 2), "gz", split_axis=2, concat_axis=2, tiled=True
    )
    fields, rows_local, cols_local = second_pass.shape
    blocks = second_pass.reshape(fields, rows_local, groups, cols_local // groups)
    return jnp.flip(blocks, 2).reshape(fields, rows_local, cols_local)


def shards(forcing, wavenumber, mean_flow, viscosity, viscosity_slope):
    vectors, components, rows_local, cols_local = forcing.shape
    rows_total = rows_local * lax.axis_size("gy")
    cols_total = cols_local * lax.axis_size("gz")
    table_y = angle_table(rows_total)
    table_z = angle_table(cols_total)
    flattened = forcing.reshape(vectors * components, rows_local, cols_local)
    first = jnp.einsum(
        "ij,fjk->fik",
        table_y,
        lax.all_to_all(flattened, "gy", split_axis=0, concat_axis=1, tiled=True),
        precision=precise,
    )
    second = jnp.einsum("ij,fjk->fik", table_y, first, precision=precise)
    grad_y = lax.all_to_all(first, "gy", split_axis=1, concat_axis=0, tiled=True)
    curve_y = lax.all_to_all(second, "gy", split_axis=1, concat_axis=0, tiled=True)
    own_start = lax.axis_index("gz") * cols_local
    own_rows = lax.dynamic_slice_in_dim(table_z, own_start, cols_local, 0)
    own_second = jnp.dot(own_rows, table_z, precision=precise, preferred_element_type=jnp.float32)
    piece = lax.all_gather(flattened, "gz", axis=2, tiled=True)
    grad_z = jnp.einsum("fyj,ij->fyi", piece, own_rows, precision=precise)
    curve_z = jnp.einsum("fyj,ij->fyi", piece, own_second, precision=precise)
    full_shape = forcing.shape
    action = apply_operator(
        forcing,
        grad_y.reshape(full_shape),
        curve_y.reshape(full_shape),
        grad_z.reshape(full_shape),
        curve_z.reshape(full_shape),
        wavenumber[0],
        mean_flow,
        viscosity,
        viscosity_slope,
    )
    y_signs = jnp.array([1.0, 1.0, -1.0, -1.0, 1.0, 1.0, 1.0, 1.0], dtype=jnp.float32)[
        :, None, None
    ]
    z_signs = jnp.array([1.0, 1.0, 1.0, 1.0, -1.0, -1.0, 1.0, 1.0], dtype=jnp.float32)[
        :, None, None
    ]
    flat_shape = (vectors * components, rows_local, cols_local)
    mirrored = mirror_rows(action.reshape(flat_shape)).reshape(full_shape)
    half_y = 0.5 * (action + y_signs * mirrored)
    mirrored = mirror_cols(half_y.reshape(flat_shape)).reshape(full_shape)
    return 0.5 * (half_y + z_signs * mirrored)


Y_SIGNS = (1, -1, 1, 1)
Z_SIGNS = (1, 1, -1, 1)
SINE_TERMS = 7


def short_sine(x):
    square = x * x
    total = jnp.full_like(x, 1.0 / math.factorial(2 * SINE_TERMS - 1) * (-1) ** (SINE_TERMS - 1))
    for k in range(SINE_TERMS - 2, -1, -1):
        total = total * square + (-1) ** k / math.factorial(2 * k + 1)
    return total * x


def half_rows_of(points, mirrored):
    half, last_index = points // 2, points - 1
    row_index = jnp.arange(half, dtype=jnp.int32)[:, None]
    col_index = jnp.arange(half, dtype=jnp.int32)[None, :]
    if mirrored:
        col_index = last_index - col_index
    unit = math.pi / (2.0 * last_index)
    sine_row = short_sine(2.0 * unit * row_index.astype(jnp.float32))
    total = row_index + col_index
    half_sum = short_sine(unit * jnp.minimum(total, 2 * last_index - total).astype(jnp.float32))
    half_diff = short_sine(unit * (row_index - col_index).astype(jnp.float32))
    parity = (1 - 2 * (total % 2)).astype(jnp.float32)
    weight = jnp.where((col_index == 0) | (col_index == last_index), 0.5, 1.0).astype(jnp.float32)
    same = row_index == col_index
    denominator = jnp.where(same, 1.0, 2.0 * half_sum * half_diff)
    return jnp.where(same, 0.0, math.pi / last_index * sine_row * parity * weight / denominator)


def parity_tables(points):
    near, far = half_rows_of(points, False), half_rows_of(points, True)
    near = near - jnp.diag(jnp.sum(near, axis=1) + jnp.sum(far, axis=1))
    even, odd = near + far, near - far
    second_even = jnp.dot(odd, even, precision=precise)
    second_odd = jnp.dot(even, odd, precision=precise)
    return even, odd, second_even, second_odd


def split2(x):
    high = x.astype(jnp.bfloat16)
    return high, (x - high.astype(jnp.float32)).astype(jnp.bfloat16)


def mxu(a, b):
    return jnp.dot(a, b, preferred_element_type=jnp.float32)


def dot3(a, b):
    a_high, a_low = split2(a)
    b_high, b_low = split2(b)
    return mxu(a_high, b_high) + (mxu(a_high, b_low) + mxu(a_low, b_high))


def exchange(size):
    i = lax.broadcasted_iota(jnp.int32, (size, size), 0)
    j = lax.broadcasted_iota(jnp.int32, (size, size), 1)
    return jnp.where(i + j == size - 1, 1.0, 0.0).astype(jnp.bfloat16)


def split3(x):
    high, rest = split2(x)
    middle = x - high.astype(jnp.float32)
    low = (middle - rest.astype(jnp.float32)).astype(jnp.bfloat16)
    return high, rest, low


def flip_lanes(x):
    width = x.shape[1]
    size = 256 if width % 256 == 0 else 128
    turn = exchange(size)
    out = []
    for start in range(width - size, -1, -size):
        high, middle, low = split3(x[:, start : start + size])
        out.append(mxu(high, turn) + (mxu(middle, turn) + mxu(low, turn)))
    return out[0] if len(out) == 1 else jnp.concatenate(out, axis=1)


def flip_rows(x):
    high, middle, low = split3(x)
    turn = exchange(x.shape[0])
    return mxu(turn, high) + (mxu(turn, middle) + mxu(turn, low))


def times_i(pair):
    return jnp.concatenate((-pair[1:2], pair[0:1]))


def action_along_z(source, grad, curve, streamwise, coefs):
    u, v, w, p = source
    stream, advect, uy, uz, vy, vz, wy, wz, nu = (coefs[k : k + 1] for k in range(9))
    out = []
    for k, (c, sy, sz) in enumerate(((u, uy, uz), (v, vy, vz), (w, wy, wz))):
        term = (
            advect * grad[k]
            - (streamwise * stream) * times_i(c)
            - (sy * v + sz * w)
            + nu * (curve[k] - streamwise * streamwise * c)
        )
        if k == 0:
            term = term - streamwise * times_i(p)
        if k == 2:
            term = term - grad[3]
        out.append(term)
    out.append(streamwise * times_i(u) + grad[2])
    return out


def body(
    groups, wave_ref, f_ref, c_ref, tz_ref, ty_ref, out_ref,
    pair, coef, far, far_coef, lines, line_coef, grad, curve, z_part, z_lines, whole, piece, outgoing,
    local, cross_s, cross_r, coef_s, coef_r, own_s, own_r, fwd_s, fwd_r, lc_s, lc_r,
    zp_s, zp_r, q_s, q_r, fin_s, fin_r,
):
    rows, cols = f_ref.shape[2], f_ref.shape[3]
    width = cols // groups
    half = rows * groups // 2
    g, h, core = lax.axis_index("gy"), lax.axis_index("gz"), lax.axis_index("vec")
    streamwise = wave_ref[0]
    peers = [lax.rem(g + d, groups) for d in range(groups)]

    barrier = pltpu.get_barrier_semaphore()
    for d in range(1, groups):
        pl.semaphore_signal(
            barrier, inc=1, device_id={"gy": peers[d]}, device_id_type=pl.DeviceIdType.MESH
        )
    pl.semaphore_signal(barrier, inc=1, device_id={"gz": 1 - h}, device_id_type=pl.DeviceIdType.MESH)
    pl.semaphore_signal(
        barrier, inc=1, device_id={"vec": 1 - core}, device_id_type=pl.DeviceIdType.MESH
    )
    pl.semaphore_wait(barrier, groups + 1)

    def remote(src, dst, send, recv, device):
        copy = pltpu.make_async_remote_copy(
            src_ref=src, dst_ref=dst, send_sem=send, recv_sem=recv,
            device_id=device, device_id_type=pl.DeviceIdType.MESH,
        )
        copy.start()
        return copy

    def here(src, dst, k):
        copy = pltpu.make_async_copy(src, dst, local.at[k])
        copy.start()
        return copy

    def block(p):
        return pl.ds(pl.multiple_of(p * width, width), width)

    def block_of(side, p):
        return block(jnp.where(side == 0, p, groups - 1 - p))

    my_rows = pl.ds(pl.multiple_of(g * rows, rows), rows)

    cross = [
        remote(
            f_ref.at[1 - h, pl.ds(2 * k, 2)], pair.at[h, pl.ds(2 * k, 2)],
            cross_s.at[k], cross_r.at[k], {"gz": 1 - h},
        )
        for k in range(4)
    ]
    own_lines = [
        remote(
            f_ref.at[h, :, :, block_of(h, peers[d])], lines.at[h, :, my_rows, :],
            own_s.at[d], own_r.at[d], {"gy": peers[d]},
        )
        for d in range(1, groups)
    ]
    share = c_ref.shape[0] // 2
    shared = pl.ds(core * share, share)
    coef_cross = remote(
        c_ref.at[shared], coef.at[h, shared], coef_s.at[0], coef_r.at[0], {"gz": 1 - h}
    )
    own_copy = here(f_ref.at[h], pair.at[h], 0)
    coef_copy = here(c_ref, coef.at[h], 1)
    line_copy = here(f_ref.at[h, :, :, block_of(h, g)], lines.at[h, :, my_rows, :], 2)
    own_copy.wait()
    forwarded, line_copies = [], [line_copy]

    def derive(k):
        near = pair[0, 2 * k : 2 * k + 2].reshape(2 * rows, cols)
        mirror = flip_lanes(pair[1, 2 * k : 2 * k + 2].reshape(2 * rows, cols))
        far[2 * k : 2 * k + 2] = mirror.reshape(2, rows, cols)
        even, odd = 0.5 * (near + mirror), 0.5 * (near - mirror)
        first, second = dot3(even, tz_ref[0]), dot3(odd, tz_ref[1])
        grad[0, 2 * k : 2 * k + 2] = (second + first).reshape(2, rows, cols)
        grad[1, 2 * k : 2 * k + 2] = (second - first).reshape(2, rows, cols)
        if k < 3:
            first, second = dot3(even, tz_ref[2]), dot3(odd, tz_ref[3])
            curve[0, 2 * k : 2 * k + 2] = (first + second).reshape(2, rows, cols)
            curve[1, 2 * k : 2 * k + 2] = (first - second).reshape(2, rows, cols)

    for k in range(4):
        two = pl.ds(2 * k, 2)
        cross[k].wait_recv()
        for d in range(1, groups):
            forwarded.append(
                remote(
                    pair.at[1 - h, two, :, block_of(1 - h, peers[d])],
                    lines.at[1 - h, two, my_rows, :],
                    fwd_s.at[k, d], fwd_r.at[k, d], {"gy": peers[d]},
                )
            )
        line_copies.append(
            here(
                pair.at[1 - h, two, :, block_of(1 - h, g)],
                lines.at[1 - h, two, my_rows, :],
                3 + k,
            )
        )
        derive(k)

    coef_copy.wait()
    coef_cross.wait_recv()
    coef_mate = remote(
        coef.at[1 - h, shared], coef.at[1 - h, shared], coef_s.at[1], coef_r.at[1], {"vec": 1 - core}
    )
    coef_mate.wait_recv()
    coef_lines = []
    for s in range(2):
        for d in range(1, groups):
            coef_lines.append(
                remote(
                    coef.at[s, pl.ds(8, 2), :, block_of(s, peers[d])],
                    line_coef.at[s, :, my_rows, :],
                    lc_s.at[s, d], lc_r.at[s, d], {"gy": peers[d]},
                )
            )
        line_copies.append(
            here(coef.at[s, pl.ds(8, 2), :, block_of(s, g)], line_coef.at[s, :, my_rows, :], 7 + s)
        )
    for k in range(9):
        far_coef[k] = flip_lanes(coef[1, k])

    @pl.loop(0, rows // 8)
    def _(step):
        at = pl.ds(pl.multiple_of(step * 8, 8), 8)

        def act(source, side, coefs):
            return action_along_z(
                [source[2 * k : 2 * k + 2, at, :] for k in range(4)],
                [grad[side, 2 * k : 2 * k + 2, at, :] for k in range(4)],
                [curve[side, 2 * k : 2 * k + 2, at, :] for k in range(3)],
                streamwise,
                coefs,
            )

        near_action = act(pair.at[0], 0, coef[0, 0:9, at, :])
        far_action = act(far, 1, far_coef[0:9, at, :])
        for k in range(4):
            z_part[2 * k : 2 * k + 2, at, :] = 0.5 * (near_action[k] + Z_SIGNS[k] * far_action[k])

    z_moves = [
        remote(
            z_part.at[:, :, block(peers[d])], z_lines.at[:, my_rows, :],
            zp_s.at[d], zp_r.at[d], {"gy": peers[d]},
        )
        for d in range(1, groups)
    ]
    z_copy = here(z_part.at[:, :, block(g)], z_lines.at[:, my_rows, :], 9)

    for copy in line_copies:
        copy.wait()
    for copy in own_lines + forwarded + coef_lines:
        copy.wait_recv()

    def join(values):
        return jnp.concatenate((values[0], values[1]), axis=1)

    for s in range(2):
        top_advect, top_nu = line_coef[s, 1, :half], line_coef[s, 0, :half]
        low = flip_rows(jnp.concatenate((line_coef[s, 0, half:], line_coef[s, 1, half:]), axis=1))
        low_nu, low_advect = low[:, :width], low[:, width:]
        top_advect, top_nu, low_advect, low_nu = (
            jnp.concatenate((x, x), axis=1) for x in (top_advect, top_nu, low_advect, low_nu)
        )

        def add(k, value, start):
            value = value if s == 0 else Z_SIGNS[k] * flip_lanes_each(value)
            for part in range(2):
                term = 0.5 * value[:, part * width : (part + 1) * width]
                if start:
                    whole[2 * k + part, :half] = term
                else:
                    whole[2 * k + part, :half] = whole[2 * k + part, :half] + term

        def flip_lanes_each(value):
            return jnp.concatenate(
                (flip_lanes(value[:, :width]), flip_lanes(value[:, width:])), axis=1
            )

        for k in range(4):
            top = join(lines[s, 2 * k : 2 * k + 2, :half, :])
            bottom = flip_rows(join(lines[s, 2 * k : 2 * k + 2, half:, :]))
            even, odd = 0.5 * (top + bottom), 0.5 * (top - bottom)
            first, second = dot3(ty_ref[0], even), dot3(ty_ref[1], odd)
            grad_top, grad_low = second + first, second - first
            if k < 3:
                first, second = dot3(ty_ref[2], even), dot3(ty_ref[3], odd)
                top_action = top_advect * grad_top + top_nu * (first + second)
                low_action = low_advect * grad_low + low_nu * (first - second)
                add(k, 0.5 * (top_action + Y_SIGNS[k] * low_action), s == 0)
            if k == 1:
                add(3, 0.5 * (grad_top + Y_SIGNS[3] * grad_low), s == 0)
            if k == 3:
                add(1, -0.5 * (grad_top + Y_SIGNS[1] * grad_low), False)

    z_copy.wait()
    for copy in z_moves:
        copy.wait_recv()
    for k in range(4):
        top = join(z_lines[2 * k : 2 * k + 2, :half, :])
        bottom = flip_rows(join(z_lines[2 * k : 2 * k + 2, half:, :]))
        quarter = join(whole[2 * k : 2 * k + 2, :half, :]) + 0.5 * (top + Y_SIGNS[k] * bottom)
        mirror = Y_SIGNS[k] * flip_rows(quarter)
        for part in range(2):
            whole[2 * k + part, :half] = quarter[:, part * width : (part + 1) * width]
            whole[2 * k + part, half:] = mirror[:, part * width : (part + 1) * width]

    results = [None]
    for d in range(1, groups):
        to_rows = pl.ds(pl.multiple_of(peers[d] * rows, rows), rows)
        results.append(
            remote(
                whole.at[:, to_rows, :], piece.at[d], q_s.at[d], q_r.at[d], {"gy": peers[d]}
            )
        )
    finals = []
    for d in range(groups):
        if d:
            results[d].wait_recv()
        owner = lax.rem(g - d + groups, groups)
        flat = (whole[:, my_rows, :] if d == 0 else piece[d]).reshape(8 * rows, width)
        mirror = flip_lanes(flat)
        flat, mirror = flat.reshape(8, rows, width), mirror.reshape(8, rows, width)
        mirror = jnp.concatenate((mirror[:4], -mirror[4:6], mirror[6:]))
        out_ref[h, :, :, block_of(h, owner)] = jnp.where(h == 0, flat, mirror)
        outgoing[d] = jnp.where(h == 0, mirror, flat)
        finals.append(
            remote(
                outgoing.at[d], out_ref.at[h, :, :, block_of(1 - h, owner)],
                fin_s.at[d], fin_r.at[d], {"gz": 1 - h},
            )
        )
    for copy in finals:
        copy.wait_recv()
    for copy in cross + own_lines + [coef_cross, coef_mate] + forwarded + coef_lines + z_moves:
        copy.wait_send()
    for copy in results[1:] + finals:
        copy.wait_send()


def paired_shards(groups, forcing, wavenumber, mean_flow, viscosity, viscosity_slope):
    vectors, components, rows, cols = forcing.shape
    width, rows_total = cols // groups, rows * groups
    coefs = jnp.concatenate(
        (
            mean_flow[0:1],
            viscosity_slope[1:2] - mean_flow[2:3],
            mean_flow[3:9],
            viscosity[None],
            viscosity_slope[0:1] - mean_flow[1:2],
        )
    )
    tables_z = jnp.stack([table.T for table in parity_tables(2 * cols)])
    tables_y = jnp.stack(parity_tables(rows_total))
    f32 = jnp.float32
    dma = pltpu.SemaphoreType.DMA
    vmem = pl.BlockSpec(memory_space=pltpu.VMEM)
    anywhere = pl.BlockSpec(memory_space=pl.ANY)
    return pl.pallas_call(
        functools.partial(body, groups),
        out_shape=jax.ShapeDtypeStruct(forcing.shape, f32),
        in_specs=[pl.BlockSpec(memory_space=pltpu.SMEM), anywhere, anywhere, vmem, vmem],
        out_specs=vmem,
        scratch_shapes=[
            pltpu.VMEM((2, 8, rows, cols), f32),
            pltpu.VMEM((2, 10, rows, cols), f32),
            pltpu.VMEM((8, rows, cols), f32),
            pltpu.VMEM((9, rows, cols), f32),
            pltpu.VMEM((2, 8, rows_total, width), f32),
            pltpu.VMEM((2, 2, rows_total, width), f32),
            pltpu.VMEM((2, 8, rows, cols), f32),
            pltpu.VMEM((2, 6, rows, cols), f32),
            pltpu.VMEM((8, rows, cols), f32),
            pltpu.VMEM((8, rows_total, width), f32),
            pltpu.VMEM((8, rows_total, width), f32),
            pltpu.VMEM((groups, 8, rows, width), f32),
            pltpu.VMEM((groups, 8, rows, width), f32),
            dma((10,)),
            dma((4,)), dma((4,)),
            dma((2,)), dma((2,)),
            dma((groups,)), dma((groups,)),
            dma((4, groups)), dma((4, groups)),
            dma((2, groups)), dma((2, groups)),
            dma((groups,)), dma((groups,)),
            dma((groups,)), dma((groups,)),
            dma((groups,)), dma((groups,)),
        ],
        compiler_params=pltpu.CompilerParams(
            collective_id=0, has_side_effects=True, vmem_limit_bytes=60 * 1024 * 1024
        ),
    )(wavenumber, forcing, coefs, tables_z, tables_y)


def shards_of(mesh):
    groups = mesh.shape["gy"]

    def run(forcing, *others):
        vectors, _, rows, cols = forcing.shape
        fits = mesh.shape["gz"] == 2 and mesh.shape["vec"] == 2 and vectors == 2
        fits = fits and groups % 2 == 0 and groups <= 4
        if fits and cols == groups * 128 and rows % 16 == 0 and rows * groups <= 512:
            return paired_shards(groups, forcing, *others)
        return shards(forcing, *others)

    return run


def solution(mesh):
    placed = (
        P(("wave", "vec"), None, "gy", "gz"),
        P("wave"),
        P(None, "gy", "gz"),
        P("gy", "gz"),
        P(None, "gy", "gz"),
    )
    return jax.shard_map(
        shards_of(mesh),
        mesh=mesh,
        in_specs=placed,
        out_specs=P(("wave", "vec"), None, "gy", "gz"),
        check_vma=False,
    )
```

```python
import functools
import math

import jax
import jax.numpy as jnp
from jax import lax
from jax.experimental import pallas as pl
from jax.experimental.pallas import tpu as pltpu
from jax.sharding import PartitionSpec as P

precise = lax.Precision.HIGHEST


def angle_table(points):
    last_index = points - 1
    row_index = jnp.arange(points, dtype=jnp.int32)[:, None]
    col_index = jnp.arange(points, dtype=jnp.int32)[None, :]
    unit = math.pi / (2.0 * last_index)
    sine_row = jnp.sin(
        2.0 * unit * jnp.minimum(row_index, last_index - row_index).astype(jnp.float32)
    )
    total = row_index + col_index
    half_sum = jnp.sin(unit * jnp.minimum(total, 2 * last_index - total).astype(jnp.float32))
    half_diff = jnp.sin(unit * (row_index - col_index).astype(jnp.float32))
    parity = (1 - 2 * (total % 2)).astype(jnp.float32)
    weight = jnp.where((col_index == 0) | (col_index == last_index), 0.5, 1.0).astype(jnp.float32)
    same = row_index == col_index
    denominator = jnp.where(same, 1.0, 2.0 * half_sum * half_diff)
    offdiag = jnp.where(same, 0.0, math.pi / last_index * sine_row * parity * weight / denominator)
    diagonal = -jnp.sum(offdiag, axis=1)
    return offdiag + jnp.diag(diagonal)


def rotate(values):
    return jnp.stack((-values[..., 1, :, :], values[..., 0, :, :]), axis=-3)


def apply_operator(
    forcing, grad_y, curve_y, grad_z, curve_z, streamwise, mean_flow, viscosity, viscosity_slope
):
    full_shape = forcing.shape
    split_shape = full_shape[:-3] + (4, 2) + full_shape[-2:]
    source = forcing.reshape(split_shape)
    grad_y = grad_y.reshape(split_shape)
    curve_y = curve_y.reshape(split_shape)
    grad_z = grad_z.reshape(split_shape)
    curve_z = curve_z.reshape(split_shape)
    velocity = source[..., :3, :, :, :]
    advection = (
        streamwise * mean_flow[0] * rotate(velocity)
        + mean_flow[1] * grad_y[..., :3, :, :, :]
        + mean_flow[2] * grad_z[..., :3, :, :, :]
    )
    slope_y = jnp.stack((mean_flow[3], mean_flow[5], mean_flow[7]))[:, None]
    slope_z = jnp.stack((mean_flow[4], mean_flow[6], mean_flow[8]))[:, None]
    produce = slope_y * source[..., 1:2, :, :, :] + slope_z * source[..., 2:3, :, :, :]
    diffuse = viscosity * (
        curve_y[..., :3, :, :, :] + curve_z[..., :3, :, :, :] - streamwise * streamwise * velocity
    )
    diffuse = (
        diffuse
        + viscosity_slope[0] * grad_y[..., :3, :, :, :]
        + viscosity_slope[1] * grad_z[..., :3, :, :, :]
    )
    pressure = jnp.stack(
        (
            streamwise * rotate(source[..., 3, :, :, :]),
            grad_y[..., 3, :, :, :],
            grad_z[..., 3, :, :, :],
        ),
        axis=-4,
    )
    momentum = -advection - produce + diffuse - pressure
    continuity = (
        streamwise * rotate(source[..., 0, :, :, :])
        + grad_y[..., 1, :, :, :]
        + grad_z[..., 2, :, :, :]
    )
    action = jnp.concatenate((momentum, continuity[..., None, :, :, :]), axis=-4)
    return action.reshape(full_shape)


def mirror_rows(values):
    groups = lax.axis_size("gy")
    first_pass = lax.all_to_all(values, "gy", split_axis=1, concat_axis=1, tiled=True)
    second_pass = lax.all_to_all(
        jnp.flip(first_pass, 1), "gy", split_axis=1, concat_axis=1, tiled=True
    )
    fields, rows_local, cols_local = second_pass.shape
    blocks = second_pass.reshape(fields, groups, rows_local // groups, cols_local)
    return jnp.flip(blocks, 1).reshape(fields, rows_local, cols_local)


def mirror_cols(values):
    groups = lax.axis_size("gz")
    first_pass = lax.all_to_all(values, "gz", split_axis=2, concat_axis=2, tiled=True)
    second_pass = lax.all_to_all(
        jnp.flip(first_pass, 2), "gz", split_axis=2, concat_axis=2, tiled=True
    )
    fields, rows_local, cols_local = second_pass.shape
    blocks = second_pass.reshape(fields, rows_local, groups, cols_local // groups)
    return jnp.flip(blocks, 2).reshape(fields, rows_local, cols_local)


def shards(forcing, wavenumber, mean_flow, viscosity, viscosity_slope):
    vectors, components, rows_local, cols_local = forcing.shape
    rows_total = rows_local * lax.axis_size("gy")
    cols_total = cols_local * lax.axis_size("gz")
    table_y = angle_table(rows_total)
    table_z = angle_table(cols_total)
    flattened = forcing.reshape(vectors * components, rows_local, cols_local)
    first = jnp.einsum(
        "ij,fjk->fik",
        table_y,
        lax.all_to_all(flattened, "gy", split_axis=0, concat_axis=1, tiled=True),
        precision=precise,
    )
    second = jnp.einsum("ij,fjk->fik", table_y, first, precision=precise)
    grad_y = lax.all_to_all(first, "gy", split_axis=1, concat_axis=0, tiled=True)
    curve_y = lax.all_to_all(second, "gy", split_axis=1, concat_axis=0, tiled=True)
    own_start = lax.axis_index("gz") * cols_local
    own_rows = lax.dynamic_slice_in_dim(table_z, own_start, cols_local, 0)
    own_second = jnp.dot(own_rows, table_z, precision=precise, preferred_element_type=jnp.float32)
    piece = lax.all_gather(flattened, "gz", axis=2, tiled=True)
    grad_z = jnp.einsum("fyj,ij->fyi", piece, own_rows, precision=precise)
    curve_z = jnp.einsum("fyj,ij->fyi", piece, own_second, precision=precise)
    full_shape = forcing.shape
    action = apply_operator(
        forcing,
        grad_y.reshape(full_shape),
        curve_y.reshape(full_shape),
        grad_z.reshape(full_shape),
        curve_z.reshape(full_shape),
        wavenumber[0],
        mean_flow,
        viscosity,
        viscosity_slope,
    )
    y_signs = jnp.array([1.0, 1.0, -1.0, -1.0, 1.0, 1.0, 1.0, 1.0], dtype=jnp.float32)[
        :, None, None
    ]
    z_signs = jnp.array([1.0, 1.0, 1.0, 1.0, -1.0, -1.0, 1.0, 1.0], dtype=jnp.float32)[
        :, None, None
    ]
    flat_shape = (vectors * components, rows_local, cols_local)
    mirrored = mirror_rows(action.reshape(flat_shape)).reshape(full_shape)
    half_y = 0.5 * (action + y_signs * mirrored)
    mirrored = mirror_cols(half_y.reshape(flat_shape)).reshape(full_shape)
    return 0.5 * (half_y + z_signs * mirrored)


Y_SIGNS = (1, -1, 1, 1)
Z_SIGNS = (1, 1, -1, 1)
SINE_TERMS = 7


def short_sine(x):
    square = x * x
    total = jnp.full_like(x, 1.0 / math.factorial(2 * SINE_TERMS - 1) * (-1) ** (SINE_TERMS - 1))
    for k in range(SINE_TERMS - 2, -1, -1):
        total = total * square + (-1) ** k / math.factorial(2 * k + 1)
    return total * x


def off_diagonal(points, row_index, col_index):
    last_index = points - 1
    unit = math.pi / (2.0 * last_index)
    sine_row = short_sine(2.0 * unit * row_index.astype(jnp.float32))
    total = row_index + col_index
    half_sum = short_sine(unit * jnp.minimum(total, 2 * last_index - total).astype(jnp.float32))
    half_diff = short_sine(unit * (row_index - col_index).astype(jnp.float32))
    parity = (1 - 2 * (total & 1)).astype(jnp.float32)
    weight = jnp.where((col_index == 0) | (col_index == last_index), 0.5, 1.0)
    same = row_index == col_index
    denominator = jnp.where(same, 1.0, 2.0 * half_sum * half_diff)
    return jnp.where(same, 0.0, math.pi / last_index * sine_row * parity * weight / denominator)


def fill_table(points, across, held, high_ref, low_ref):
    half, step = points // 2, 16

    def indices(chunk):
        down = chunk * step + lax.broadcasted_iota(jnp.int32, (step, half), 0)
        along = lax.broadcasted_iota(jnp.int32, (step, half), 1)
        return (along, down) if across else (down, along)

    def fill(chunk, total):
        row, col = indices(chunk)
        near, far = off_diagonal(points, row, col), off_diagonal(points, row, points - 1 - col)
        even, odd = near + far, near - far
        at = pl.ds(pl.multiple_of(chunk * step, step), step)
        if not across:
            own = jnp.where(row == col, jnp.sum(even, axis=1, keepdims=True), 0.0)
            even, odd = even - own, odd - own
        held[0, at, :] = even
        held[1, at, :] = odd
        return total + even

    total = lax.fori_loop(0, half // step, fill, jnp.zeros((step, half), jnp.float32))
    total = jnp.sum(total, axis=0, keepdims=True)

    @pl.loop(0, half // step)
    def _(chunk):
        row, col = indices(chunk)
        at = pl.ds(pl.multiple_of(chunk * step, step), step)
        for k in range(2):
            values = held[k, at, :]
            if across:
                values = values - jnp.where(row == col, total, 0.0)
            high_ref[k, at, :], low_ref[k, at, :] = split2(values)


def split2(x):
    high = x.astype(jnp.bfloat16)
    return high, (x - high.astype(jnp.float32)).astype(jnp.bfloat16)


def mxu(a, b):
    return jnp.dot(a, b, preferred_element_type=jnp.float32)


def dot3(a, high, low):
    a_high, a_low = split2(a)
    return mxu(a_high, high) + (mxu(a_high, low) + mxu(a_low, high))


def dot3_left(high, low, b):
    b_high, b_low = split2(b)
    return mxu(high, b_high) + (mxu(low, b_high) + mxu(high, b_low))


def exchange(size):
    i = lax.broadcasted_iota(jnp.int32, (size, size), 0)
    j = lax.broadcasted_iota(jnp.int32, (size, size), 1)
    return jnp.where(i + j == size - 1, 1.0, 0.0).astype(jnp.bfloat16)


def split3(x):
    high, rest = split2(x)
    middle = x - high.astype(jnp.float32)
    low = (middle - rest.astype(jnp.float32)).astype(jnp.bfloat16)
    return high, rest, low


def flip_lanes(x):
    width = x.shape[1]
    size = 256 if width % 256 == 0 else 128
    turn = exchange(size)
    out = []
    for start in range(width - size, -1, -size):
        high, middle, low = split3(x[:, start : start + size])
        out.append(mxu(high, turn) + (mxu(middle, turn) + mxu(low, turn)))
    return out[0] if len(out) == 1 else jnp.concatenate(out, axis=1)


def flip_rows(x):
    high, middle, low = split3(x)
    turn = exchange(x.shape[0])
    return mxu(turn, high) + (mxu(turn, middle) + mxu(turn, low))


def times_i(pair):
    return jnp.concatenate((-pair[1:2], pair[0:1]))


def action_along_z(source, grad, curve, streamwise, coefs):
    u, v, w, p = source
    stream, advect, uy, uz, vy, vz, wy, wz, nu = (coefs[k : k + 1] for k in range(9))
    out = []
    for k, (c, sy, sz) in enumerate(((u, uy, uz), (v, vy, vz), (w, wy, wz))):
        term = (
            advect * grad[k]
            - (streamwise * stream) * times_i(c)
            - (sy * v + sz * w)
            + nu * (curve[k] - streamwise * streamwise * c)
        )
        if k == 0:
            term = term - streamwise * times_i(p)
        if k == 2:
            term = term - grad[3]
        out.append(term)
    out.append(streamwise * times_i(u) + grad[2])
    return out


def body(
    groups, wave_ref, f_ref, c_ref, out_ref,
    held_z, high_z, low_z, held_y, high_y, low_y,
    pair, coef, far, far_coef, lines, line_coef, grad, curve, z_part, z_lines, whole, piece, outgoing,
    local, cross_s, cross_r, coef_s, coef_r, own_s, own_r, fwd_s, fwd_r, lc_s, lc_r, lm_s, lm_r,
    zp_s, zp_r, q_s, q_r, fin_s, fin_r,
):
    rows, cols = f_ref.shape[2], f_ref.shape[3]
    width = cols // groups
    half = rows * groups // 2
    g, h, core = lax.axis_index("gy"), lax.axis_index("gz"), lax.axis_index("vec")
    streamwise = wave_ref[0]
    peers = [lax.rem(g + d, groups) for d in range(groups)]

    barrier = pltpu.get_barrier_semaphore()
    for d in range(1, groups):
        pl.semaphore_signal(
            barrier, inc=1, device_id={"gy": peers[d]}, device_id_type=pl.DeviceIdType.MESH
        )
    pl.semaphore_signal(barrier, inc=1, device_id={"gz": 1 - h}, device_id_type=pl.DeviceIdType.MESH)
    pl.semaphore_signal(
        barrier, inc=1, device_id={"vec": 1 - core}, device_id_type=pl.DeviceIdType.MESH
    )
    pl.semaphore_wait(barrier, groups + 1)

    def remote(src, dst, send, recv, device):
        copy = pltpu.make_async_remote_copy(
            src_ref=src, dst_ref=dst, send_sem=send, recv_sem=recv,
            device_id=device, device_id_type=pl.DeviceIdType.MESH,
        )
        copy.start()
        return copy

    def here(src, dst, k):
        copy = pltpu.make_async_copy(src, dst, local.at[k])
        copy.start()
        return copy

    def block(p):
        return pl.ds(pl.multiple_of(p * width, width), width)

    def block_of(side, p):
        return block(jnp.where(side == 0, p, groups - 1 - p))

    my_rows = pl.ds(pl.multiple_of(g * rows, rows), rows)

    share = c_ref.shape[0] // 2
    shared = pl.ds(core * share, share)
    coef_cross = remote(
        c_ref.at[shared], coef.at[h, shared], coef_s.at[0], coef_r.at[0], {"gz": 1 - h}
    )
    cross = [
        remote(
            f_ref.at[1 - h, pl.ds(2 * k, 2)], pair.at[h, pl.ds(2 * k, 2)],
            cross_s.at[k], cross_r.at[k], {"gz": 1 - h},
        )
        for k in range(4)
    ]
    own_lines = [
        remote(
            f_ref.at[h, :, :, block_of(h, peers[d])], lines.at[h, :, my_rows, :],
            own_s.at[d], own_r.at[d], {"gy": peers[d]},
        )
        for d in range(1, groups)
    ]
    own_copy = here(f_ref.at[h], pair.at[h], 0)
    coef_copy = here(c_ref, coef.at[h], 1)
    line_copy = here(f_ref.at[h, :, :, block_of(h, g)], lines.at[h, :, my_rows, :], 2)
    forwarded, line_copies = [], [line_copy]
    fill_table(2 * cols, True, held_z, high_z, low_z)
    fill_table(rows * groups, False, held_y, high_y, low_y)

    coef_copy.wait()
    coef_cross.wait_recv()
    coef_mate = remote(
        coef.at[1 - h, shared], coef.at[1 - h, shared], coef_s.at[1], coef_r.at[1], {"vec": 1 - core}
    )
    coef_mate.wait_recv()
    coef_lines = []
    for s in range(2):
        for d in range(1, groups):
            coef_lines.append(
                remote(
                    coef.at[s, 8 + core, :, block_of(s, peers[d])],
                    line_coef.at[s, core, my_rows, :],
                    lc_s.at[s, d], lc_r.at[s, d], {"gy": peers[d]},
                )
            )
    coef_copies = [
        here(coef.at[s, 8 + core, :, block_of(s, g)], line_coef.at[s, core, my_rows, :], 7 + s)
        for s in range(2)
    ]
    for k in range(9):
        far_coef[k] = flip_lanes(coef[1, k])
    own_copy.wait()

    def derive(k):
        near = pair[0, 2 * k : 2 * k + 2].reshape(2 * rows, cols)
        mirror = flip_lanes(pair[1, 2 * k : 2 * k + 2].reshape(2 * rows, cols))
        far[2 * k : 2 * k + 2] = mirror.reshape(2, rows, cols)
        even, odd = 0.5 * (near + mirror), 0.5 * (near - mirror)
        first = dot3(even, high_z[0], low_z[0])
        second = dot3(odd, high_z[1], low_z[1])
        grad[0, 2 * k : 2 * k + 2] = (second + first).reshape(2, rows, cols)
        grad[1, 2 * k : 2 * k + 2] = (second - first).reshape(2, rows, cols)
        if k < 3:
            first, second = (
                dot3(first, high_z[1], low_z[1]),
                dot3(second, high_z[0], low_z[0]),
            )
            curve[0, 2 * k : 2 * k + 2] = (first + second).reshape(2, rows, cols)
            curve[1, 2 * k : 2 * k + 2] = (first - second).reshape(2, rows, cols)

    for k in range(4):
        two = pl.ds(2 * k, 2)
        cross[k].wait_recv()
        for d in range(1, groups):
            forwarded.append(
                remote(
                    pair.at[1 - h, two, :, block_of(1 - h, peers[d])],
                    lines.at[1 - h, two, my_rows, :],
                    fwd_s.at[k, d], fwd_r.at[k, d], {"gy": peers[d]},
                )
            )
        line_copies.append(
            here(
                pair.at[1 - h, two, :, block_of(1 - h, g)],
                lines.at[1 - h, two, my_rows, :],
                3 + k,
            )
        )
        derive(k)

    for copy in coef_copies:
        copy.wait()
    for copy in coef_lines:
        copy.wait_recv()
    coef_mates = [
        remote(
            line_coef.at[s, core], line_coef.at[s, core], lm_s.at[s], lm_r.at[s], {"vec": 1 - core}
        )
        for s in range(2)
    ]

    @pl.loop(0, rows // 8)
    def _(step):
        at = pl.ds(pl.multiple_of(step * 8, 8), 8)

        def act(source, side, coefs):
            return action_along_z(
                [source[2 * k : 2 * k + 2, at, :] for k in range(4)],
                [grad[side, 2 * k : 2 * k + 2, at, :] for k in range(4)],
                [curve[side, 2 * k : 2 * k + 2, at, :] for k in range(3)],
                streamwise,
                coefs,
            )

        near_action = act(pair.at[0], 0, coef[0, 0:9, at, :])
        far_action = act(far, 1, far_coef[0:9, at, :])
        for k in range(4):
            z_part[2 * k : 2 * k + 2, at, :] = 0.5 * (near_action[k] + Z_SIGNS[k] * far_action[k])

    z_moves, z_copies = [], []
    for k in range(4):
        two = pl.ds(2 * k, 2)
        z_moves.append(
            [
                remote(
                    z_part.at[two, :, block(peers[d])], z_lines.at[two, my_rows, :],
                    zp_s.at[k, d], zp_r.at[k, d], {"gy": peers[d]},
                )
                for d in range(1, groups)
            ]
        )
        z_copies.append(here(z_part.at[two, :, block(g)], z_lines.at[two, my_rows, :], 9 + k))

    for copy in line_copies:
        copy.wait()
    for copy in own_lines + forwarded + coef_mates:
        copy.wait_recv()

    def join(values):
        return jnp.concatenate((values[0], values[1]), axis=1)

    for s in range(2):
        top_advect, top_nu = line_coef[s, 1, :half], line_coef[s, 0, :half]
        low = flip_rows(jnp.concatenate((line_coef[s, 0, half:], line_coef[s, 1, half:]), axis=1))
        low_nu, low_advect = low[:, :width], low[:, width:]
        top_advect, top_nu, low_advect, low_nu = (
            jnp.concatenate((x, x), axis=1) for x in (top_advect, top_nu, low_advect, low_nu)
        )

        def add(k, value, start):
            value = value if s == 0 else Z_SIGNS[k] * flip_lanes_each(value)
            for part in range(2):
                term = 0.5 * value[:, part * width : (part + 1) * width]
                if start:
                    whole[2 * k + part, :half] = term
                else:
                    whole[2 * k + part, :half] = whole[2 * k + part, :half] + term

        def flip_lanes_each(value):
            return jnp.concatenate(
                (flip_lanes(value[:, :width]), flip_lanes(value[:, width:])), axis=1
            )

        for k in range(4):
            top = join(lines[s, 2 * k : 2 * k + 2, :half, :])
            bottom = flip_rows(join(lines[s, 2 * k : 2 * k + 2, half:, :]))
            even, odd = 0.5 * (top + bottom), 0.5 * (top - bottom)
            first = dot3_left(high_y[0], low_y[0], even)
            second = dot3_left(high_y[1], low_y[1], odd)
            grad_top, grad_low = second + first, second - first
            if k < 3:
                first, second = (
                    dot3_left(high_y[1], low_y[1], first),
                    dot3_left(high_y[0], low_y[0], second),
                )
                top_action = top_advect * grad_top + top_nu * (first + second)
                low_action = low_advect * grad_low + low_nu * (first - second)
                add(k, 0.5 * (top_action + Y_SIGNS[k] * low_action), s == 0)
            if k == 1:
                add(3, 0.5 * (grad_top + Y_SIGNS[3] * grad_low), s == 0)
            if k == 3:
                add(1, -0.5 * (grad_top + Y_SIGNS[1] * grad_low), False)

    results, finals = [], []

    def finish(k):
        two = slice(2 * k, 2 * k + 2)
        for d in range(groups):
            if d:
                results[k][d - 1].wait_recv()
            owner = lax.rem(g - d + groups, groups)
            flat = (whole[two, my_rows, :] if d == 0 else piece[d, two]).reshape(2 * rows, width)
            mirror = Z_SIGNS[k] * flip_lanes(flat)
            flat, mirror = flat.reshape(2, rows, width), mirror.reshape(2, rows, width)
            out_ref[h, two, :, block_of(h, owner)] = jnp.where(h == 0, flat, mirror)
            outgoing[d, two] = jnp.where(h == 0, mirror, flat)
            finals.append(
                remote(
                    outgoing.at[d, pl.ds(2 * k, 2)],
                    out_ref.at[h, pl.ds(2 * k, 2), :, block_of(1 - h, owner)],
                    fin_s.at[k, d], fin_r.at[k, d], {"gz": 1 - h},
                )
            )

    for k in range(4):
        z_copies[k].wait()
        for copy in z_moves[k]:
            copy.wait_recv()
        top = join(z_lines[2 * k : 2 * k + 2, :half, :])
        bottom = flip_rows(join(z_lines[2 * k : 2 * k + 2, half:, :]))
        quarter = join(whole[2 * k : 2 * k + 2, :half, :]) + 0.5 * (top + Y_SIGNS[k] * bottom)
        mirror = Y_SIGNS[k] * flip_rows(quarter)
        for part in range(2):
            whole[2 * k + part, :half] = quarter[:, part * width : (part + 1) * width]
            whole[2 * k + part, half:] = mirror[:, part * width : (part + 1) * width]
        two = pl.ds(2 * k, 2)
        results.append(
            [
                remote(
                    whole.at[two, pl.ds(pl.multiple_of(peers[d] * rows, rows), rows), :],
                    piece.at[d, two],
                    q_s.at[k, d], q_r.at[k, d], {"gy": peers[d]},
                )
                for d in range(1, groups)
            ]
        )
        if k:
            finish(k - 1)
    finish(3)
    for copy in finals:
        copy.wait_recv()
    for copy in cross + own_lines + [coef_cross, coef_mate] + forwarded + coef_lines + coef_mates:
        copy.wait_send()
    for copy in sum(z_moves, []) + sum(results, []) + finals:
        copy.wait_send()


def paired_shards(groups, forcing, wavenumber, mean_flow, viscosity, viscosity_slope):
    vectors, components, rows, cols = forcing.shape
    width, rows_total = cols // groups, rows * groups
    coefs = jnp.concatenate(
        (
            mean_flow[0:1],
            viscosity_slope[1:2] - mean_flow[2:3],
            mean_flow[3:9],
            viscosity[None],
            viscosity_slope[0:1] - mean_flow[1:2],
        )
    )
    f32, bf16 = jnp.float32, jnp.bfloat16
    half = rows_total // 2
    dma = pltpu.SemaphoreType.DMA
    vmem = pl.BlockSpec(memory_space=pltpu.VMEM)
    anywhere = pl.BlockSpec(memory_space=pl.ANY)
    return pl.pallas_call(
        functools.partial(body, groups),
        out_shape=jax.ShapeDtypeStruct(forcing.shape, f32),
        in_specs=[pl.BlockSpec(memory_space=pltpu.SMEM), anywhere, anywhere],
        out_specs=vmem,
        scratch_shapes=[
            pltpu.VMEM((2, cols, cols), f32),
            pltpu.VMEM((2, cols, cols), bf16),
            pltpu.VMEM((2, cols, cols), bf16),
            pltpu.VMEM((2, half, half), f32),
            pltpu.VMEM((2, half, half), bf16),
            pltpu.VMEM((2, half, half), bf16),
            pltpu.VMEM((2, 8, rows, cols), f32),
            pltpu.VMEM((2, 10, rows, cols), f32),
            pltpu.VMEM((8, rows, cols), f32),
            pltpu.VMEM((9, rows, cols), f32),
            pltpu.VMEM((2, 8, rows_total, width), f32),
            pltpu.VMEM((2, 2, rows_total, width), f32),
            pltpu.VMEM((2, 8, rows, cols), f32),
            pltpu.VMEM((2, 6, rows, cols), f32),
            pltpu.VMEM((8, rows, cols), f32),
            pltpu.VMEM((8, rows_total, width), f32),
            pltpu.VMEM((8, rows_total, width), f32),
            pltpu.VMEM((groups, 8, rows, width), f32),
            pltpu.VMEM((groups, 8, rows, width), f32),
            dma((13,)),
            dma((4,)), dma((4,)),
            dma((2,)), dma((2,)),
            dma((groups,)), dma((groups,)),
            dma((4, groups)), dma((4, groups)),
            dma((2, groups)), dma((2, groups)),
            dma((2,)), dma((2,)),
            dma((4, groups)), dma((4, groups)),
            dma((4, groups)), dma((4, groups)),
            dma((4, groups)), dma((4, groups)),
        ],
        compiler_params=pltpu.CompilerParams(
            collective_id=0, has_side_effects=True, vmem_limit_bytes=60 * 1024 * 1024
        ),
    )(wavenumber, forcing, coefs)


def shards_of(mesh):
    groups = mesh.shape["gy"]

    def run(forcing, *others):
        vectors, _, rows, cols = forcing.shape
        fits = mesh.shape["gz"] == 2 and mesh.shape["vec"] == 2 and vectors == 2
        fits = fits and groups % 2 == 0 and groups <= 4
        if fits and cols == groups * 128 and rows % 16 == 0 and rows * groups <= 512:
            return paired_shards(groups, forcing, *others)
        return shards(forcing, *others)

    return run


def solution(mesh):
    placed = (
        P(("wave", "vec"), None, "gy", "gz"),
        P("wave"),
        P(None, "gy", "gz"),
        P("gy", "gz"),
        P(None, "gy", "gz"),
    )
    return jax.shard_map(
        shards_of(mesh),
        mesh=mesh,
        in_specs=placed,
        out_specs=P(("wave", "vec"), None, "gy", "gz"),
        check_vma=False,
    )
```

```python
import functools
import math

import jax
import jax.numpy as jnp
from jax import lax
from jax.experimental import pallas as pl
from jax.experimental.pallas import tpu as pltpu
from jax.sharding import PartitionSpec as P

precise = lax.Precision.HIGHEST


def angle_table(points):
    last_index = points - 1
    row_index = jnp.arange(points, dtype=jnp.int32)[:, None]
    col_index = jnp.arange(points, dtype=jnp.int32)[None, :]
    unit = math.pi / (2.0 * last_index)
    sine_row = jnp.sin(
        2.0 * unit * jnp.minimum(row_index, last_index - row_index).astype(jnp.float32)
    )
    total = row_index + col_index
    half_sum = jnp.sin(unit * jnp.minimum(total, 2 * last_index - total).astype(jnp.float32))
    half_diff = jnp.sin(unit * (row_index - col_index).astype(jnp.float32))
    parity = (1 - 2 * (total % 2)).astype(jnp.float32)
    weight = jnp.where((col_index == 0) | (col_index == last_index), 0.5, 1.0).astype(jnp.float32)
    same = row_index == col_index
    denominator = jnp.where(same, 1.0, 2.0 * half_sum * half_diff)
    offdiag = jnp.where(same, 0.0, math.pi / last_index * sine_row * parity * weight / denominator)
    diagonal = -jnp.sum(offdiag, axis=1)
    return offdiag + jnp.diag(diagonal)


def rotate(values):
    return jnp.stack((-values[..., 1, :, :], values[..., 0, :, :]), axis=-3)


def apply_operator(
    forcing, grad_y, curve_y, grad_z, curve_z, streamwise, mean_flow, viscosity, viscosity_slope
):
    full_shape = forcing.shape
    split_shape = full_shape[:-3] + (4, 2) + full_shape[-2:]
    source = forcing.reshape(split_shape)
    grad_y = grad_y.reshape(split_shape)
    curve_y = curve_y.reshape(split_shape)
    grad_z = grad_z.reshape(split_shape)
    curve_z = curve_z.reshape(split_shape)
    velocity = source[..., :3, :, :, :]
    advection = (
        streamwise * mean_flow[0] * rotate(velocity)
        + mean_flow[1] * grad_y[..., :3, :, :, :]
        + mean_flow[2] * grad_z[..., :3, :, :, :]
    )
    slope_y = jnp.stack((mean_flow[3], mean_flow[5], mean_flow[7]))[:, None]
    slope_z = jnp.stack((mean_flow[4], mean_flow[6], mean_flow[8]))[:, None]
    produce = slope_y * source[..., 1:2, :, :, :] + slope_z * source[..., 2:3, :, :, :]
    diffuse = viscosity * (
        curve_y[..., :3, :, :, :] + curve_z[..., :3, :, :, :] - streamwise * streamwise * velocity
    )
    diffuse = (
        diffuse
        + viscosity_slope[0] * grad_y[..., :3, :, :, :]
        + viscosity_slope[1] * grad_z[..., :3, :, :, :]
    )
    pressure = jnp.stack(
        (
            streamwise * rotate(source[..., 3, :, :, :]),
            grad_y[..., 3, :, :, :],
            grad_z[..., 3, :, :, :],
        ),
        axis=-4,
    )
    momentum = -advection - produce + diffuse - pressure
    continuity = (
        streamwise * rotate(source[..., 0, :, :, :])
        + grad_y[..., 1, :, :, :]
        + grad_z[..., 2, :, :, :]
    )
    action = jnp.concatenate((momentum, continuity[..., None, :, :, :]), axis=-4)
    return action.reshape(full_shape)


def mirror_rows(values):
    groups = lax.axis_size("gy")
    first_pass = lax.all_to_all(values, "gy", split_axis=1, concat_axis=1, tiled=True)
    second_pass = lax.all_to_all(
        jnp.flip(first_pass, 1), "gy", split_axis=1, concat_axis=1, tiled=True
    )
    fields, rows_local, cols_local = second_pass.shape
    blocks = second_pass.reshape(fields, groups, rows_local // groups, cols_local)
    return jnp.flip(blocks, 1).reshape(fields, rows_local, cols_local)


def mirror_cols(values):
    groups = lax.axis_size("gz")
    first_pass = lax.all_to_all(values, "gz", split_axis=2, concat_axis=2, tiled=True)
    second_pass = lax.all_to_all(
        jnp.flip(first_pass, 2), "gz", split_axis=2, concat_axis=2, tiled=True
    )
    fields, rows_local, cols_local = second_pass.shape
    blocks = second_pass.reshape(fields, rows_local, groups, cols_local // groups)
    return jnp.flip(blocks, 2).reshape(fields, rows_local, cols_local)


def shards(forcing, wavenumber, mean_flow, viscosity, viscosity_slope):
    vectors, components, rows_local, cols_local = forcing.shape
    rows_total = rows_local * lax.axis_size("gy")
    cols_total = cols_local * lax.axis_size("gz")
    table_y = angle_table(rows_total)
    table_z = angle_table(cols_total)
    flattened = forcing.reshape(vectors * components, rows_local, cols_local)
    first = jnp.einsum(
        "ij,fjk->fik",
        table_y,
        lax.all_to_all(flattened, "gy", split_axis=0, concat_axis=1, tiled=True),
        precision=precise,
    )
    second = jnp.einsum("ij,fjk->fik", table_y, first, precision=precise)
    grad_y = lax.all_to_all(first, "gy", split_axis=1, concat_axis=0, tiled=True)
    curve_y = lax.all_to_all(second, "gy", split_axis=1, concat_axis=0, tiled=True)
    own_start = lax.axis_index("gz") * cols_local
    own_rows = lax.dynamic_slice_in_dim(table_z, own_start, cols_local, 0)
    own_second = jnp.dot(own_rows, table_z, precision=precise, preferred_element_type=jnp.float32)
    piece = lax.all_gather(flattened, "gz", axis=2, tiled=True)
    grad_z = jnp.einsum("fyj,ij->fyi", piece, own_rows, precision=precise)
    curve_z = jnp.einsum("fyj,ij->fyi", piece, own_second, precision=precise)
    full_shape = forcing.shape
    action = apply_operator(
        forcing,
        grad_y.reshape(full_shape),
        curve_y.reshape(full_shape),
        grad_z.reshape(full_shape),
        curve_z.reshape(full_shape),
        wavenumber[0],
        mean_flow,
        viscosity,
        viscosity_slope,
    )
    y_signs = jnp.array([1.0, 1.0, -1.0, -1.0, 1.0, 1.0, 1.0, 1.0], dtype=jnp.float32)[
        :, None, None
    ]
    z_signs = jnp.array([1.0, 1.0, 1.0, 1.0, -1.0, -1.0, 1.0, 1.0], dtype=jnp.float32)[
        :, None, None
    ]
    flat_shape = (vectors * components, rows_local, cols_local)
    mirrored = mirror_rows(action.reshape(flat_shape)).reshape(full_shape)
    half_y = 0.5 * (action + y_signs * mirrored)
    mirrored = mirror_cols(half_y.reshape(flat_shape)).reshape(full_shape)
    return 0.5 * (half_y + z_signs * mirrored)


Y_SIGNS = (1, -1, 1, 1)
Z_SIGNS = (1, 1, -1, 1)
Z_COEFS = (0, 11, 3, 4, 5, 6, 7, 8, 9)
SINE_TERMS = 7


def short_sine(x):
    square = x * x
    total = jnp.full_like(x, 1.0 / math.factorial(2 * SINE_TERMS - 1) * (-1) ** (SINE_TERMS - 1))
    for k in range(SINE_TERMS - 2, -1, -1):
        total = total * square + (-1) ** k / math.factorial(2 * k + 1)
    return total * x


def off_diagonal(points, row_index, col_index):
    last_index = points - 1
    unit = math.pi / (2.0 * last_index)
    sine_row = short_sine(2.0 * unit * row_index.astype(jnp.float32))
    total = row_index + col_index
    half_sum = short_sine(unit * jnp.minimum(total, 2 * last_index - total).astype(jnp.float32))
    half_diff = short_sine(unit * (row_index - col_index).astype(jnp.float32))
    parity = (1 - 2 * (total & 1)).astype(jnp.float32)
    weight = jnp.where((col_index == 0) | (col_index == last_index), 0.5, 1.0)
    same = row_index == col_index
    denominator = jnp.where(same, 1.0, 2.0 * half_sum * half_diff)
    return jnp.where(same, 0.0, math.pi / last_index * sine_row * parity * weight / denominator)


def fill_table(points, across, held, high_ref, low_ref):
    half, step = points // 2, 16

    def indices(chunk):
        down = chunk * step + lax.broadcasted_iota(jnp.int32, (step, half), 0)
        along = lax.broadcasted_iota(jnp.int32, (step, half), 1)
        return (along, down) if across else (down, along)

    def fill(chunk, total):
        row, col = indices(chunk)
        near, far = off_diagonal(points, row, col), off_diagonal(points, row, points - 1 - col)
        even, odd = near + far, near - far
        at = pl.ds(pl.multiple_of(chunk * step, step), step)
        if not across:
            own = jnp.where(row == col, jnp.sum(even, axis=1, keepdims=True), 0.0)
            even, odd = even - own, odd - own
        held[0, at, :] = even
        held[1, at, :] = odd
        return total + even

    total = lax.fori_loop(0, half // step, fill, jnp.zeros((step, half), jnp.float32))
    total = jnp.sum(total, axis=0, keepdims=True)

    @pl.loop(0, half // step)
    def _(chunk):
        row, col = indices(chunk)
        at = pl.ds(pl.multiple_of(chunk * step, step), step)
        for k in range(2):
            values = held[k, at, :]
            if across:
                values = values - jnp.where(row == col, total, 0.0)
            high_ref[k, at, :], low_ref[k, at, :] = split2(values)


def split2(x):
    high = x.astype(jnp.bfloat16)
    return high, (x - high.astype(jnp.float32)).astype(jnp.bfloat16)


def mxu(a, b):
    return jnp.dot(a, b, preferred_element_type=jnp.float32)


def dot3(a, high, low):
    a_high, a_low = split2(a)
    return mxu(a_high, high) + (mxu(a_high, low) + mxu(a_low, high))


def dot3_left(high, low, b):
    b_high, b_low = split2(b)
    return mxu(high, b_high) + (mxu(low, b_high) + mxu(high, b_low))


def exchange(size):
    i = lax.broadcasted_iota(jnp.int32, (size, size), 0)
    j = lax.broadcasted_iota(jnp.int32, (size, size), 1)
    return jnp.where(i + j == size - 1, 1.0, 0.0).astype(jnp.bfloat16)


def split3(x):
    high, rest = split2(x)
    middle = x - high.astype(jnp.float32)
    low = (middle - rest.astype(jnp.float32)).astype(jnp.bfloat16)
    return high, rest, low


def flip_lanes(x):
    width = x.shape[1]
    size = 256 if width % 256 == 0 else 128
    turn = exchange(size)
    out = []
    for start in range(width - size, -1, -size):
        high, middle, low = split3(x[:, start : start + size])
        out.append(mxu(high, turn) + (mxu(middle, turn) + mxu(low, turn)))
    return out[0] if len(out) == 1 else jnp.concatenate(out, axis=1)


def flip_rows(x):
    high, middle, low = split3(x)
    turn = exchange(x.shape[0])
    return mxu(turn, high) + (mxu(turn, middle) + mxu(turn, low))


def times_i(pair):
    return jnp.concatenate((-pair[1:2], pair[0:1]))


def action_along_z(source, grad, curve, streamwise, coefs):
    u, v, w, p = source
    stream, advect, uy, uz, vy, vz, wy, wz, nu = (coefs[k : k + 1] for k in Z_COEFS)
    out = []
    for k, (c, sy, sz) in enumerate(((u, uy, uz), (v, vy, vz), (w, wy, wz))):
        term = (
            advect * grad[k]
            - (streamwise * stream) * times_i(c)
            - (sy * v + sz * w)
            + nu * (curve[k] - streamwise * streamwise * c)
        )
        if k == 0:
            term = term - streamwise * times_i(p)
        if k == 2:
            term = term - grad[3]
        out.append(term)
    out.append(streamwise * times_i(u) + grad[2])
    return out


def body(
    groups, wave_ref, f_ref, flow_ref, nu_ref, slope_ref, out_ref,
    held_z, high_z, low_z, held_y, high_y, low_y,
    pair, coef, far, far_coef, lines, line_coef, grad, curve, z_part, z_lines, whole, piece, kept, outgoing,
    local, cross_s, cross_r, coef_s, coef_r, own_s, own_r, fwd_s, fwd_r, lc_s, lc_r, lm_s, lm_r,
    zp_s, zp_r, q_s, q_r, fin_s, fin_r,
):
    rows, cols = f_ref.shape[2], f_ref.shape[3]
    width = cols // groups
    half = rows * groups // 2
    g, h, core = lax.axis_index("gy"), lax.axis_index("gz"), lax.axis_index("vec")
    streamwise = wave_ref[0]
    peers = [lax.rem(g + d, groups) for d in range(groups)]

    barrier = pltpu.get_barrier_semaphore()
    for d in range(1, groups):
        pl.semaphore_signal(
            barrier, inc=1, device_id={"gy": peers[d]}, device_id_type=pl.DeviceIdType.MESH
        )
    pl.semaphore_signal(barrier, inc=1, device_id={"gz": 1 - h}, device_id_type=pl.DeviceIdType.MESH)
    pl.semaphore_signal(
        barrier, inc=1, device_id={"vec": 1 - core}, device_id_type=pl.DeviceIdType.MESH
    )
    pl.semaphore_wait(barrier, groups + 1)

    def remote(src, dst, send, recv, device):
        copy = pltpu.make_async_remote_copy(
            src_ref=src, dst_ref=dst, send_sem=send, recv_sem=recv,
            device_id=device, device_id_type=pl.DeviceIdType.MESH,
        )
        copy.start()
        return copy

    def here(src, dst, k):
        copy = pltpu.make_async_copy(src, dst, local.at[k])
        copy.start()
        return copy

    def block(p):
        return pl.ds(pl.multiple_of(p * width, width), width)

    def block_of(side, p):
        return block(jnp.where(side == 0, p, groups - 1 - p))

    my_rows = pl.ds(pl.multiple_of(g * rows, rows), rows)

    own_lines = [
        remote(
            f_ref.at[h, :, :, block_of(h, peers[d])], lines.at[h, :, my_rows, :],
            own_s.at[d], own_r.at[d], {"gy": peers[d]},
        )
        for d in range(1, groups)
    ]
    coef_copies = [
        here(flow_ref, coef.at[h, pl.ds(0, 9)], 1),
        here(nu_ref, coef.at[h, 9], 13),
        here(slope_ref, coef.at[h, pl.ds(10, 2)], 14),
    ]
    for copy in coef_copies:
        copy.wait()
    shared = pl.ds(core * 6, 6)
    coef_cross = remote(
        coef.at[h, shared], coef.at[h, shared], coef_s.at[0], coef_r.at[0], {"gz": 1 - h}
    )
    cross = [
        remote(
            f_ref.at[1 - h, pl.ds(2 * k, 2)], pair.at[h, pl.ds(2 * k, 2)],
            cross_s.at[k], cross_r.at[k], {"gz": 1 - h},
        )
        for k in range(4)
    ]
    own_copy = here(f_ref.at[h], pair.at[h], 0)
    line_copy = here(f_ref.at[h, :, :, block_of(h, g)], lines.at[h, :, my_rows, :], 2)
    forwarded, line_copies = [], [line_copy]
    fill_table(2 * cols, True, held_z, high_z, low_z)
    fill_table(rows * groups, False, held_y, high_y, low_y)

    coef_cross.wait_recv()
    coef_mate = remote(
        coef.at[1 - h, shared], coef.at[1 - h, shared], coef_s.at[1], coef_r.at[1], {"vec": 1 - core}
    )
    coef_mate.wait_recv()
    coef_cross.wait_send()
    coef_mate.wait_send()
    for s in range(2):
        for k in range(2):
            coef[s, 10 + k] = coef[s, 10 + k] - coef[s, 1 + k]
    coef_lines = []
    for s in range(2):
        for d in range(1, groups):
            coef_lines.append(
                remote(
                    coef.at[s, 9 + core, :, block_of(s, peers[d])],
                    line_coef.at[s, core, my_rows, :],
                    lc_s.at[s, d], lc_r.at[s, d], {"gy": peers[d]},
                )
            )
    coef_copies = [
        here(coef.at[s, 9 + core, :, block_of(s, g)], line_coef.at[s, core, my_rows, :], 7 + s)
        for s in range(2)
    ]
    for k in Z_COEFS:
        far_coef[k] = flip_lanes(coef[1, k])
    own_copy.wait()

    def derive(k):
        near = pair[0, 2 * k : 2 * k + 2].reshape(2 * rows, cols)
        mirror = flip_lanes(pair[1, 2 * k : 2 * k + 2].reshape(2 * rows, cols))
        far[2 * k : 2 * k + 2] = mirror.reshape(2, rows, cols)
        even, odd = 0.5 * (near + mirror), 0.5 * (near - mirror)
        first = dot3(even, high_z[0], low_z[0])
        second = dot3(odd, high_z[1], low_z[1])
        grad[0, 2 * k : 2 * k + 2] = (second + first).reshape(2, rows, cols)
        grad[1, 2 * k : 2 * k + 2] = (second - first).reshape(2, rows, cols)
        if k < 3:
            first, second = (
                dot3(first, high_z[1], low_z[1]),
                dot3(second, high_z[0], low_z[0]),
            )
            curve[0, 2 * k : 2 * k + 2] = (first + second).reshape(2, rows, cols)
            curve[1, 2 * k : 2 * k + 2] = (first - second).reshape(2, rows, cols)

    for k in range(4):
        two = pl.ds(2 * k, 2)
        cross[k].wait_recv()
        for d in range(1, groups):
            forwarded.append(
                remote(
                    pair.at[1 - h, two, :, block_of(1 - h, peers[d])],
                    lines.at[1 - h, two, my_rows, :],
                    fwd_s.at[k, d], fwd_r.at[k, d], {"gy": peers[d]},
                )
            )
        line_copies.append(
            here(
                pair.at[1 - h, two, :, block_of(1 - h, g)],
                lines.at[1 - h, two, my_rows, :],
                3 + k,
            )
        )
        derive(k)

    for copy in coef_copies:
        copy.wait()
    for copy in coef_lines:
        copy.wait_recv()
    coef_mates = [
        remote(
            line_coef.at[s, core], line_coef.at[s, core], lm_s.at[s], lm_r.at[s], {"vec": 1 - core}
        )
        for s in range(2)
    ]

    @pl.loop(0, rows // 8)
    def _(step):
        at = pl.ds(pl.multiple_of(step * 8, 8), 8)

        def act(source, side, coefs):
            return action_along_z(
                [source[2 * k : 2 * k + 2, at, :] for k in range(4)],
                [grad[side, 2 * k : 2 * k + 2, at, :] for k in range(4)],
                [curve[side, 2 * k : 2 * k + 2, at, :] for k in range(3)],
                streamwise,
                coefs,
            )

        near_action = act(pair.at[0], 0, coef[0, :, at, :])
        far_action = act(far, 1, far_coef[:, at, :])
        for k in range(4):
            z_part[2 * k : 2 * k + 2, at, :] = 0.5 * (near_action[k] + Z_SIGNS[k] * far_action[k])

    z_moves, z_copies = [], []
    for k in range(4):
        two = pl.ds(2 * k, 2)
        z_moves.append(
            [
                remote(
                    z_part.at[two, :, block(peers[d])], z_lines.at[two, my_rows, :],
                    zp_s.at[k, d], zp_r.at[k, d], {"gy": peers[d]},
                )
                for d in range(1, groups)
            ]
        )
        z_copies.append(here(z_part.at[two, :, block(g)], z_lines.at[two, my_rows, :], 9 + k))

    for copy in line_copies:
        copy.wait()
    for copy in own_lines + forwarded + coef_mates:
        copy.wait_recv()

    def join(values):
        return jnp.concatenate((values[0], values[1]), axis=1)

    for s in range(2):
        top_advect, top_nu = line_coef[s, 1, :half], line_coef[s, 0, :half]
        low = flip_rows(jnp.concatenate((line_coef[s, 0, half:], line_coef[s, 1, half:]), axis=1))
        low_nu, low_advect = low[:, :width], low[:, width:]
        top_advect, top_nu, low_advect, low_nu = (
            jnp.concatenate((x, x), axis=1) for x in (top_advect, top_nu, low_advect, low_nu)
        )

        def add(k, value, start):
            value = value if s == 0 else Z_SIGNS[k] * flip_lanes_each(value)
            for part in range(2):
                term = 0.5 * value[:, part * width : (part + 1) * width]
                if start:
                    whole[2 * k + part, :half] = term
                else:
                    whole[2 * k + part, :half] = whole[2 * k + part, :half] + term

        def flip_lanes_each(value):
            return jnp.concatenate(
                (flip_lanes(value[:, :width]), flip_lanes(value[:, width:])), axis=1
            )

        for k in range(4):
            top = join(lines[s, 2 * k : 2 * k + 2, :half, :])
            bottom = flip_rows(join(lines[s, 2 * k : 2 * k + 2, half:, :]))
            even, odd = 0.5 * (top + bottom), 0.5 * (top - bottom)
            first = dot3_left(high_y[0], low_y[0], even)
            second = dot3_left(high_y[1], low_y[1], odd)
            grad_top, grad_low = second + first, second - first
            if k < 3:
                first, second = (
                    dot3_left(high_y[1], low_y[1], first),
                    dot3_left(high_y[0], low_y[0], second),
                )
                top_action = top_advect * grad_top + top_nu * (first + second)
                low_action = low_advect * grad_low + low_nu * (first - second)
                add(k, 0.5 * (top_action + Y_SIGNS[k] * low_action), s == 0)
            if k == 1:
                add(3, 0.5 * (grad_top + Y_SIGNS[3] * grad_low), s == 0)
            if k == 3:
                add(1, -0.5 * (grad_top + Y_SIGNS[1] * grad_low), False)

    results, finals, stored = [], [], []

    def finish(k):
        for c in (2 * k, 2 * k + 1):
            for d in range(groups):
                if d:
                    results[c][d - 1].wait_recv()
                owner = lax.rem(g - d + groups, groups)
                flat = whole[c, my_rows, :] if d == 0 else piece[d, c]
                mirror = Z_SIGNS[k] * flip_lanes(flat)
                kept[c, :, block_of(h, owner)] = jnp.where(h == 0, flat, mirror)
                outgoing[d, c] = jnp.where(h == 0, mirror, flat)
                finals.append(
                    remote(
                        outgoing.at[d, c], out_ref.at[h, c, :, block_of(1 - h, owner)],
                        fin_s.at[c, d], fin_r.at[c, d], {"gz": 1 - h},
                    )
                )
            stored.append(here(kept.at[c], out_ref.at[h, c], 15 + c))

    for k in range(4):
        z_copies[k].wait()
        for copy in z_moves[k]:
            copy.wait_recv()
        top = join(z_lines[2 * k : 2 * k + 2, :half, :])
        bottom = flip_rows(join(z_lines[2 * k : 2 * k + 2, half:, :]))
        quarter = join(whole[2 * k : 2 * k + 2, :half, :]) + 0.5 * (top + Y_SIGNS[k] * bottom)
        mirror = Y_SIGNS[k] * flip_rows(quarter)
        for part in range(2):
            whole[2 * k + part, :half] = quarter[:, part * width : (part + 1) * width]
            whole[2 * k + part, half:] = mirror[:, part * width : (part + 1) * width]
        for c in (2 * k, 2 * k + 1):
            results.append(
                [
                    remote(
                        whole.at[c, pl.ds(pl.multiple_of(peers[d] * rows, rows), rows), :],
                        piece.at[d, c],
                        q_s.at[c, d], q_r.at[c, d], {"gy": peers[d]},
                    )
                    for d in range(1, groups)
                ]
            )
        if k:
            finish(k - 1)
    finish(3)
    for copy in stored:
        copy.wait()
    for copy in finals:
        copy.wait_recv()
    for copy in cross + own_lines + forwarded + coef_lines + coef_mates:
        copy.wait_send()
    for copy in sum(z_moves, []) + sum(results, []) + finals:
        copy.wait_send()


def paired_shards(groups, forcing, wavenumber, mean_flow, viscosity, viscosity_slope):
    vectors, components, rows, cols = forcing.shape
    width, rows_total = cols // groups, rows * groups
    f32, bf16 = jnp.float32, jnp.bfloat16
    half = rows_total // 2
    dma = pltpu.SemaphoreType.DMA
    anywhere = pl.BlockSpec(memory_space=pl.ANY)
    return pl.pallas_call(
        functools.partial(body, groups),
        out_shape=jax.ShapeDtypeStruct(forcing.shape, f32),
        in_specs=[pl.BlockSpec(memory_space=pltpu.SMEM), anywhere, anywhere, anywhere, anywhere],
        out_specs=anywhere,
        scratch_shapes=[
            pltpu.VMEM((2, cols, cols), f32),
            pltpu.VMEM((2, cols, cols), bf16),
            pltpu.VMEM((2, cols, cols), bf16),
            pltpu.VMEM((2, half, half), f32),
            pltpu.VMEM((2, half, half), bf16),
            pltpu.VMEM((2, half, half), bf16),
            pltpu.VMEM((2, 8, rows, cols), f32),
            pltpu.VMEM((2, 12, rows, cols), f32),
            pltpu.VMEM((8, rows, cols), f32),
            pltpu.VMEM((12, rows, cols), f32),
            pltpu.VMEM((2, 8, rows_total, width), f32),
            pltpu.VMEM((2, 2, rows_total, width), f32),
            pltpu.VMEM((2, 8, rows, cols), f32),
            pltpu.VMEM((2, 6, rows, cols), f32),
            pltpu.VMEM((8, rows, cols), f32),
            pltpu.VMEM((8, rows_total, width), f32),
            pltpu.VMEM((8, rows_total, width), f32),
            pltpu.VMEM((groups, 8, rows, width), f32),
            pltpu.VMEM((8, rows, cols), f32),
            pltpu.VMEM((groups, 8, rows, width), f32),
            dma((23,)),
            dma((4,)), dma((4,)),
            dma((2,)), dma((2,)),
            dma((groups,)), dma((groups,)),
            dma((4, groups)), dma((4, groups)),
            dma((2, groups)), dma((2, groups)),
            dma((2,)), dma((2,)),
            dma((4, groups)), dma((4, groups)),
            dma((8, groups)), dma((8, groups)),
            dma((8, groups)), dma((8, groups)),
        ],
        compiler_params=pltpu.CompilerParams(
            collective_id=0, has_side_effects=True, vmem_limit_bytes=60 * 1024 * 1024
        ),
    )(wavenumber, forcing, mean_flow, viscosity, viscosity_slope)


def shards_of(mesh):
    groups = mesh.shape["gy"]

    def run(forcing, *others):
        vectors, _, rows, cols = forcing.shape
        fits = mesh.shape["gz"] == 2 and mesh.shape["vec"] == 2 and vectors == 2
        fits = fits and groups % 2 == 0 and groups <= 4
        if fits and cols == groups * 128 and rows % 16 == 0 and rows * groups <= 512:
            return paired_shards(groups, forcing, *others)
        return shards(forcing, *others)

    return run


def solution(mesh):
    placed = (
        P(("wave", "vec"), None, "gy", "gz"),
        P("wave"),
        P(None, "gy", "gz"),
        P("gy", "gz"),
        P(None, "gy", "gz"),
    )
    return jax.shard_map(
        shards_of(mesh),
        mesh=mesh,
        in_specs=placed,
        out_specs=P(("wave", "vec"), None, "gy", "gz"),
        check_vma=False,
    )
```
